128 devices in a mesh: elem: 16 (over x, y), lev: 8 (over z, core).
Axes of the slice: x: 4, y: 4, z: 4, core: 2. Of those that a mesh axis runs over, the one named last changes fastest.
Arguments:
- right_side: float32 [128, 16, 16384], P('lev', None, 'elem'), may hold values from -150 to 150, as said below
- metric: float32 [3, 16, 16384], P(None, None, 'elem'), may hold values from -0.3 to 0.5, as said below
- mass_weight: float32 [16, 16384], P(None, 'elem'), may hold values from 0.5 to 2
- helmholtz: float32 [128], P('lev'), may hold values from 0.5 to 2
- vertical: float32 [128, 16384], P('lev', 'elem'), may hold values from 0.5 to 2
- block_inverse: float32 [16, 8, 8, 16384], P('lev', None, None, 'elem'), may hold values from 0 to 1.1, as said below
- edge_neighbour: int32 [16384, 4], P('elem'), may hold values from -1 to 65535, as said below
- edge_flip: int32 [16384, 4], P('elem'), may hold values from 0 to 1, as said below
- corner_neighbour: int32 [16384, 4, 3], P('elem'), may hold values from -1 to 65535, as said below
- element_count: int32 [16], P('elem'), may hold values from 512 to 1024, as said below
Outputs:
- solution: float32 [128, 16, 16384], P('lev', None, 'elem')
- residual: float32 [128, 16, 16384], P('lev', None, 'elem')
- direction: float32 [128, 16, 16384], P('lev', None, 'elem')
The draws below stay inside these ranges and needn't reach their ends.
Inputs may be any that keep to these rules, and one draw needn't show every extreme that they name: `right_side`: grows along the element slots and the levels; not promised to be smooth. At every node metric[0] > 0, metric[2] > 0 and metric[1] squared is below metric[0] metric[2]. Each block_inverse[k, :, :, g] is symmetric positive definite. edge_neighbour[g, j] = 4 h + i where side i of element slot h (device index along elem times 1024 plus slot) meets side j of slot g, or -1 on the patch border and on empty slots; the relation is mutual. Slots that meet by a side or a corner lie on the same device of elem or on one next to it: on the device before among its last 129 live slots, on the device after among its first 129. `edge_flip`: 1 where the two sides that meet run in opposite node orders, 0 elsewhere and on empty slots. corner_neighbour[g, k] lists the corners 4 h + c of the other element slots that share corner k of slot g, padded with -1; the relation is mutual. The live slots of device d are its first element_count[d]; the counts add up to 12288, and some device is full.
All inputs are finite; a program needn't handle non-finite values.
Results may differ from the reference program's by a relative error of at most 0.008.
Values sent between devices are 32-bit elements; how exact they have to be, the bound alone decides.
No kernel may reach another device: no remote copies, remote signals or barrier semaphores. Data moves between devices by JAX's collectives and lax.ppermute only.
A program may use at most 128 MiB of HBM per device.

```python
import math
import jax
import jax.numpy as jnp
import numpy as np
from jax import lax

LEVELS = 128
BLOCK = 8
NODES = 16
COLUMNS = 128
SLOTS = 1024
ITERATIONS = 3
ELEMENTS = 16384
PATCH_ROWS = 96
BLOCKS = 16
N_ELEM = 16


SIDE_ROW = np.array([-1, 0, 1, 0])


SIDE_COLUMN = np.array([0, 1, 0, -1])


EDGE_NODE_A = np.array([1, 3, 1, 0])


EDGE_NODE_B = np.array([0, 1, 3, 1])


CORNER_ROW = np.array([[0, -1, -1], [0, -1, -1], [0, 1, 1], [0, 1, 1]])


CORNER_COLUMN = np.array([[-1, -1, 0], [1, 1, 0], [1, 1, 0], [-1, -1, 0]])


CORNER_OTHER = np.array([[1, 2, 3], [0, 3, 2], [3, 0, 1], [2, 1, 0]])


def lattice(grid_row, column, turned, node_a, node_b):
    moved_a = jnp.where(turned == 0, node_a, jnp.where(turned == 1, 3 - node_b, jnp.where(turned == 2, 3 - node_a, node_b)))
    moved_b = jnp.where(turned == 0, node_b, jnp.where(turned == 1, node_a, jnp.where(turned == 2, 3 - node_b, 3 - node_a)))
    return (3 * column + moved_a, 3 * grid_row + moved_b)


def patch_layout(key):
    key_pair = jax.random.fold_in(key, 101)
    key_sign = jax.random.fold_in(key, 102)
    key_full = jax.random.fold_in(key, 103)
    key_turn = jax.random.fold_in(key, 104)
    pair_total = N_ELEM // 2
    quarter = SLOTS // 4
    odd_shift = 2 * jax.random.randint(key_pair, (pair_total,), 0, quarter // 2) + 1
    signs = 2 * jax.random.randint(key_sign, (pair_total,), 0, 2) - 1
    chosen = jax.random.randint(key_full, (), 0, pair_total)
    shifted = jnp.where(jnp.arange(pair_total) == chosen, quarter, odd_shift) * signs
    middle = 3 * SLOTS // 4
    counts = jnp.stack([middle + shifted, middle - shifted], axis=1).reshape(N_ELEM).astype(jnp.int32)
    starts = jnp.cumsum(counts) - counts
    patch_total = PATCH_ROWS * COLUMNS
    turns = jax.random.randint(key_turn, (patch_total,), 0, 4)
    slot_ids = jnp.arange(N_ELEM * SLOTS)
    holder = slot_ids // SLOTS
    within = slot_ids % SLOTS
    living = within < counts[holder]
    place = jnp.minimum(starts[holder] + within, patch_total - 1)
    grid_row = place // COLUMNS
    column = place % COLUMNS
    turned = turns[place]
    every_place = jnp.arange(patch_total)
    owning = jnp.sum((every_place[:, None] >= starts[None, :]).astype(jnp.int32), axis=1) - 1
    labels = owning * SLOTS + every_place - starts[owning]
    edges = []
    flips = []
    for side_here in range(4):
        side_global = (side_here + turned) % 4
        other_row = grid_row + jnp.asarray(SIDE_ROW)[side_global]
        other_column = column + jnp.asarray(SIDE_COLUMN)[side_global]
        inside = living & (other_row >= 0) & (other_row < PATCH_ROWS) & (other_column >= 0) & (other_column < COLUMNS)
        other_place = jnp.clip(other_row * COLUMNS + other_column, 0, patch_total - 1)
        other_turn = turns[other_place]
        other_side = (side_global + 2 - other_turn) % 4
        mine = lattice(grid_row, column, turned, int(EDGE_NODE_A[side_here]), int(EDGE_NODE_B[side_here]))
        theirs = lattice(other_row, other_column, other_turn, jnp.asarray(EDGE_NODE_A)[other_side], jnp.asarray(EDGE_NODE_B)[other_side])
        matching = (mine[0] == theirs[0]) & (mine[1] == theirs[1])
        edges.append(jnp.where(inside, labels[other_place] * 4 + other_side, -1))
        flips.append(jnp.where(inside & jnp.logical_not(matching), 1, 0))
    corners = []
    for corner_here in range(4):
        corner_global = (corner_here + turned) % 4
        sharers = []
        for other_id in range(3):
            other_row = grid_row + jnp.asarray(CORNER_ROW)[corner_global, other_id]
            other_column = column + jnp.asarray(CORNER_COLUMN)[corner_global, other_id]
            inside = living & (other_row >= 0) & (other_row < PATCH_ROWS) & (other_column >= 0) & (other_column < COLUMNS)
            other_place = jnp.clip(other_row * COLUMNS + other_column, 0, patch_total - 1)
            other_turn = turns[other_place]
            other_corner = (jnp.asarray(CORNER_OTHER)[corner_global, other_id] - other_turn) % 4
            sharers.append(jnp.where(inside, labels[other_place] * 4 + other_corner, -1))
        corners.append(jnp.stack(sharers, axis=1))
    edge_table = jnp.stack(edges, axis=1).astype(jnp.int32)
    flip_table = jnp.stack(flips, axis=1).astype(jnp.int32)
    corner_table = jnp.stack(corners, axis=1).astype(jnp.int32)
    return (counts, edge_table, flip_table, corner_table)


def draw_element_count(key, part):
    layout = patch_layout(key)
    return layout[0]


def draw_edge_neighbour(key, part):
    layout = patch_layout(key)
    return layout[1]


def draw_edge_flip(key, part):
    layout = patch_layout(key)
    return layout[2]


def draw_corner_neighbour(key, part):
    layout = patch_layout(key)
    return layout[3]


def draw_right_side(key, part):
    key = jax.random.fold_in(key, 5)
    key_noise, key_elem, key_level = jax.random.split(key, 3)
    shape = (LEVELS, NODES, ELEMENTS)
    level_pos = jnp.arange(LEVELS, dtype=jnp.float32)[:, None, None] / LEVELS
    slot_pos = jnp.arange(ELEMENTS, dtype=jnp.float32)[None, None, :] / ELEMENTS
    rising = jnp.exp(math.log(3.0) * 0.5 * (level_pos + slot_pos))
    level_scale = jnp.exp(jax.random.uniform(key_level, (LEVELS, 1, 1), jnp.float32, 0.0, math.log(3.0)))
    slot_scale = jnp.exp(jax.random.uniform(key_elem, (1, 1, ELEMENTS), jnp.float32, 0.0, math.log(4.0)))
    noise = jnp.clip(jax.random.normal(key_noise, shape, jnp.float32), -4.0, 4.0)
    values = 0.5 * rising * slot_scale * level_scale * noise
    return values.astype(jnp.float32)


def draw_metric(key, part):
    key = jax.random.fold_in(key, 7)
    key_first, key_second, key_cross = jax.random.split(key, 3)
    shape = (NODES, ELEMENTS)
    lowest = math.log(0.1)
    highest = math.log(0.4)
    first = jnp.exp(jax.random.uniform(key_first, shape, jnp.float32, lowest, highest))
    second = jnp.exp(jax.random.uniform(key_second, shape, jnp.float32, lowest, highest))
    cross = 0.6 * jax.random.uniform(key_cross, shape, jnp.float32, -1.0, 1.0) * jnp.sqrt(first * second)
    return jnp.stack([first, cross, second]).astype(jnp.float32)


def draw_block_inverse(key, part):
    key = jax.random.fold_in(key, 9)
    key_decay, key_extra, key_noise = jax.random.split(key, 3)
    decay = jax.random.uniform(key_decay, (BLOCKS, 1, 1, ELEMENTS), jnp.float32, 0.85, 0.97)
    rows = jnp.arange(BLOCK, dtype=jnp.float32)[None, :, None, None]
    cols = jnp.arange(BLOCK, dtype=jnp.float32)[None, None, :, None]
    distance = jnp.abs(rows - cols)
    decayed = jnp.exp(distance * jnp.log(decay))
    extra = jax.random.uniform(key_extra, (BLOCKS, BLOCK, 1, ELEMENTS), jnp.float32, 0.5, 1.0) * (distance == 0.0)
    raw = jax.random.uniform(key_noise, (BLOCKS, BLOCK, BLOCK, ELEMENTS), jnp.float32, -0.05, 0.05)
    noise = 0.5 * (raw + jnp.transpose(raw, (0, 2, 1, 3)))
    return (0.5 * (decayed + extra + noise)).astype(jnp.float32)


def level_of(own_key, dims, cuts, low, top_value):
    def one(dim, parts):
        heights = jax.random.uniform(jax.random.fold_in(jax.random.fold_in(own_key, 6), dim), (parts,), jnp.float32, low / len(cuts), top_value / len(cuts))
        return jnp.repeat(jnp.exp(heights), dims[dim] // parts).reshape((-1,) + (1,) * (len(dims) - dim - 1))

    factor_of = one(*cuts[0])
    for cut in cuts[1:]:
        factor_of = factor_of * one(*cut)
    return factor_of


def setup_inputs(seed: int = 0) -> dict:
    keys = jax.random.split(jax.random.key(seed), 11)
    return {
        "right_side": draw_right_side(jax.random.fold_in(keys[10], 71), 0),
        "metric": draw_metric(jax.random.fold_in(keys[10], 71), 0),
        "mass_weight": jnp.clip(jnp.exp(math.log(2.0) - 1.3862944 * jax.random.uniform(keys[2], (NODES, ELEMENTS), jnp.float32) ** level_of(keys[2], (NODES, ELEMENTS), ((1, 16),), -0.2, 0.2)), 0.5, 2.0),
        "helmholtz": jnp.clip(jnp.exp(math.log(2.0) - 1.3862944 * jax.random.uniform(keys[3], (LEVELS,), jnp.float32) ** level_of(keys[3], (LEVELS,), ((0, 8),), -0.2, 0.2)), 0.5, 2.0),
        "vertical": jnp.clip(jnp.exp(math.log(2.0) - 1.3862944 * jax.random.uniform(keys[4], (LEVELS, ELEMENTS), jnp.float32) ** level_of(keys[4], (LEVELS, ELEMENTS), ((0, 8), (1, 16)), -0.2, 0.2)), 0.5, 2.0),
        "block_inverse": draw_block_inverse(jax.random.fold_in(keys[10], 71), 0),
        "edge_neighbour": draw_edge_neighbour(jax.random.fold_in(keys[10], 71), 0),
        "edge_flip": draw_edge_flip(jax.random.fold_in(keys[10], 71), 0),
        "corner_neighbour": draw_corner_neighbour(jax.random.fold_in(keys[10], 71), 0),
        "element_count": draw_element_count(jax.random.fold_in(keys[10], 71), 0),
    }


PENALTY = 2.0

def gradient_table():
    root = 1.0 / math.sqrt(5.0)
    points = [-1.0, -root, root, 1.0]
    legendre = [0.5 * (5.0 * p * p * p - 3.0 * p) for p in points]
    matrix = [[0.0 for col in range(4)] for row in range(4)]
    for row in range(4):
        for col in range(4):
            if row != col:
                matrix[row][col] = legendre[row] / (legendre[col] * (points[row] - points[col]))
    matrix[0][0] = -3.0
    matrix[3][3] = 3.0
    derivative = np.array(matrix)
    return np.concatenate([np.kron(np.eye(4), derivative), np.kron(derivative, np.eye(4))], axis=0)

def stiffness(field, metric):
    table = jnp.asarray(gradient_table(), dtype=field.dtype)
    gradients = jnp.einsum('kn,lne->lke', table, field, precision=lax.Precision.HIGHEST)
    along_x = gradients[:, :16]
    along_y = gradients[:, 16:]
    flux_x = metric[0] * along_x + metric[1] * along_y
    flux_y = metric[1] * along_x + metric[2] * along_y
    return jnp.einsum('kn,lke->lne', table, jnp.concatenate([flux_x, flux_y], axis=1), precision=lax.Precision.HIGHEST)

def boundary_values(field):
    picks = [1, 2, 7, 11, 13, 14, 4, 8, 0, 3, 15, 12]
    return jnp.concatenate([field[:, node:node + 1] for node in picks], axis=1)

def edge_sources(edge_neighbour, edge_flip, locate, columns_total):
    present = edge_neighbour >= 0
    target = jnp.where(present, edge_neighbour, 0)
    element = target // 4
    side_there = target % 4
    column = jnp.where(present, locate(element), 0)
    indices = []
    presence = []
    for side_here in range(4):
        for node_here in range(2):
            node_there = jnp.where(edge_flip[:, side_here] == 1, 1 - node_here, node_here)
            indices.append((2 * side_there[:, side_here] + node_there) * columns_total + column[:, side_here])
            presence.append(present[:, side_here])
    return (jnp.stack(indices).astype(jnp.int32), jnp.stack(presence).astype(jnp.float32))

def corner_sources(corner_neighbour, locate, columns_total):
    present = corner_neighbour >= 0
    target = jnp.where(present, corner_neighbour, 0)
    element = target // 4
    corner = target % 4
    column = jnp.where(present, locate(element), 0)
    position = (8 + corner) * columns_total + column
    return (jnp.transpose(position, (1, 2, 0)).astype(jnp.int32), jnp.transpose(present, (1, 2, 0)).astype(jnp.float32))

def neighbour_values(pooled, position):
    flattened = pooled.reshape(pooled.shape[0], -1)
    picked = jnp.take(flattened, position.reshape(-1), axis=1)
    return picked.reshape((pooled.shape[0],) + position.shape)

def penalty_term(border_values, edge_values, edge_weight, corner_values, corner_weight):
    edge_jump = edge_weight * (border_values[:, :8] - edge_values)
    corner_jump = lax.optimization_barrier(jnp.sum(corner_weight * (border_values[:, 8:, None] - corner_values), axis=2))
    zero_row = jnp.zeros_like(border_values[:, :1])
    node_rows = [corner_jump[:, 0:1], edge_jump[:, 0:1], edge_jump[:, 1:2], corner_jump[:, 1:2], edge_jump[:, 6:7], zero_row, zero_row, edge_jump[:, 2:3], edge_jump[:, 7:8], zero_row, zero_row, edge_jump[:, 3:4], corner_jump[:, 3:4], edge_jump[:, 4:5], edge_jump[:, 5:6], corner_jump[:, 2:3]]
    return jnp.concatenate(node_rows, axis=1)

def column_solve(field, inverse, coupling):
    blocks = field.reshape(inverse.shape[0], inverse.shape[1], field.shape[1], field.shape[2])

    def forward(carried, pieces):
        level_block, matrix, linking = pieces
        lifted = jnp.concatenate([level_block[:1] + carried[None], level_block[1:]], axis=0)
        solved = jnp.einsum('ije,jke->ike', matrix, lifted, precision=lax.Precision.HIGHEST)
        return (linking[None, :] * solved[-1], solved)
    initial = jnp.zeros(field.shape[1:], field.dtype)
    unused, solved = lax.scan(forward, initial, (blocks, inverse, coupling))

    def backward(carried, pieces):
        level_block, matrix, linking = pieces
        corrected = level_block + (linking[None, :] * carried)[None] * matrix[:, -1][:, None, :]
        return (corrected[0], corrected)
    unused, result = lax.scan(backward, initial, (solved, inverse, coupling), reverse=True)
    return result.reshape(field.shape)

def same_column(element):
    return element

def reference(right_side, metric, mass_weight, helmholtz, vertical, block_inverse, edge_neighbour, edge_flip, corner_neighbour, element_count):
    element_total = right_side.shape[2]
    slot_ids = jnp.arange(element_total, dtype=jnp.int32)
    living = slot_ids % SLOTS < element_count[slot_ids // SLOTS]
    source = jnp.where(living[None, None, :], right_side, jnp.zeros_like(right_side))
    edge_index, edge_weight = edge_sources(edge_neighbour, edge_flip, same_column, element_total)
    corner_index, corner_weight = corner_sources(corner_neighbour, same_column, element_total)
    coupling = vertical[BLOCK - 1::BLOCK]

    def operate(field):
        border_values = boundary_values(field)
        edge_values = neighbour_values(border_values, edge_index)
        corner_values = neighbour_values(border_values, corner_index)
        jump_term = penalty_term(border_values, edge_values, edge_weight, corner_values, corner_weight)
        above = jnp.concatenate([field[1:], jnp.zeros_like(field[:1])], axis=0)
        level_flux = vertical[:, None, :] * (field - above)
        below_flux = jnp.concatenate([jnp.zeros_like(level_flux[:1]), level_flux[:-1]], axis=0)
        diagonal = helmholtz[:, None, None] * mass_weight[None] * field
        return diagonal + stiffness(field, metric) + PENALTY * jump_term + level_flux - below_flux
    smoothed = column_solve(source, block_inverse, coupling)
    residual = source
    direction = smoothed
    norm_now = jnp.sum(residual * smoothed)
    solution = jnp.zeros_like(source)
    for iteration in range(ITERATIONS):
        applied = operate(direction)
        step_size = norm_now / jnp.sum(direction * applied)
        solution = solution + step_size * direction
        residual = residual - step_size * applied
        smoothed = column_solve(residual, block_inverse, coupling)
        norm_next = jnp.sum(residual * smoothed)
        direction = smoothed + norm_next / norm_now * direction
        norm_now = norm_next
    return (solution, residual, direction)
```

```python
import math

import jax
import jax.numpy as jnp
import numpy as np
from jax import lax
from jax.experimental import pallas as pl
from jax.experimental.pallas import tpu as pltpu
from jax.sharding import PartitionSpec as P

COLUMNS = 128
ITERATIONS = 3
BORDER = COLUMNS + 1
LANES = 128
LEVELS = 16
NODES = 16
GROUPS = 8
PENALTY = 2.0
ABSENT = 15 * LANES
VMEM_BYTES = 40 * 1024 * 1024
F32 = jnp.float32
BF16 = jnp.bfloat16


def gradient_table():
    root = 1.0 / math.sqrt(5.0)
    points = [-1.0, -root, root, 1.0]
    legendre = [0.5 * (5.0 * p * p * p - 3.0 * p) for p in points]
    matrix = [[0.0 for col in range(4)] for row in range(4)]
    for row in range(4):
        for col in range(4):
            if row != col:
                matrix[row][col] = legendre[row] / (legendre[col] * (points[row] - points[col]))
    matrix[0][0] = -3.0
    matrix[3][3] = 3.0
    derivative = np.array(matrix)
    return np.kron(np.eye(4), derivative), np.kron(derivative, np.eye(4))


def stacked_tables():
    along_x, along_y = gradient_table()
    table = np.concatenate([np.kron(np.eye(8), along_x), np.kron(np.eye(8), along_y)], axis=0)
    table = jnp.asarray(table, F32)
    high = table.astype(BF16)
    low = (table - high.astype(F32)).astype(BF16)
    return jnp.stack([high, low]), jnp.stack([high.T, low.T])


def lane_take(values, index):
    return jnp.take_along_axis(values, index, axis=1, mode="promise_in_bounds")


def row_take(values, index):
    return jnp.take_along_axis(values, index, axis=0, mode="promise_in_bounds")


def iotas():
    rows = lax.broadcasted_iota(jnp.int32, (8, LANES), 0)
    lanes = lax.broadcasted_iota(jnp.int32, (8, LANES), 1)
    return rows, lanes


def by_row(rows, values):
    index = jnp.zeros_like(rows)
    for row, value in enumerate(values):
        if value:
            index = jnp.where(rows == row, value, index)
    return index


def edge_table(low, high, rows):
    from_low = row_take(low, by_row(rows, [1, 2, 7, 0, 0, 0, 4, 0]))
    from_high = row_take(high, by_row(rows, [0, 0, 0, 3, 5, 6, 0, 0]))
    use_low = (rows < 3) | (rows == 6)
    return jnp.where(use_low, from_low, from_high)


def corner_table(low, high, low_next, high_next, rows):
    index_low = by_row(rows, [0, 3, 0, 0, 0, 3, 0, 0])
    index_high = by_row(rows, [0, 0, 7, 4, 0, 0, 7, 4])
    first = jnp.where(rows < 2, row_take(low, index_low), row_take(high, index_high))
    second = jnp.where(rows < 6, row_take(low_next, index_low), row_take(high_next, index_high))
    return jnp.where(rows < 4, first, second)


def store_tables(load, rows, put):
    for pair in range(LEVELS // 2):
        even = load(2 * pair)
        odd = load(2 * pair + 1)
        put(2 * pair, edge_table(even[:8], even[8:], rows))
        put(2 * pair + 1, edge_table(odd[:8], odd[8:], rows))
        put(LEVELS + pair, corner_table(even[:8], even[8:], odd[:8], odd[8:], rows))


def gather_pick(table, first_tile, ints, counts, lists, per_list, tile, edges, corners, pick):
    rows, lanes = iotas()
    for item in range(16):
        source = jnp.broadcast_to(ints[item : item + 1, :], (8, LANES))
        lane = jnp.bitwise_and(source, LANES - 1)
        holder = lax.shift_right_logical(source, 7)
        slot = item * 8 + tile
        members = range(LEVELS) if item < 4 else range(LEVELS, LEVELS + 8)

        def step(turn, sums, lane=lane, holder=holder, slot=slot, members=members):
            which = lists[slot * per_list + turn]
            hit = holder == which
            column = pl.multiple_of((which - first_tile) * LANES, LANES)
            return tuple(
                jnp.where(hit, lane_take(table[member, :, pl.ds(column, LANES)], lane), value)
                for member, value in zip(members, sums)
            )

        start = tuple(jnp.zeros((8, LANES), F32) for member in members)
        sums = lax.fori_loop(0, counts[slot], step, start)
        for position, value in enumerate(sums):
            if item < 4:
                edges[item, position] = value
            else:
                corners[item - 4, position] = value
    low_index = ints[16:24, :]
    high_index = ints[24:32, :]
    for level in range(LEVELS):
        pair, half = level // 2, level % 2
        low = jnp.where(
            (rows == 1) | (rows == 2),
            row_take(edges[0, level], low_index),
            jnp.where(
                rows == 7, row_take(edges[1, level], low_index), row_take(edges[3, level], low_index)
            ),
        )
        low = jnp.where((rows == 5) | (rows == 6), 0.0, low)
        high = jnp.where(
            rows == 3,
            row_take(edges[1, level], high_index),
            jnp.where(rows == 0, row_take(edges[3, level], high_index), row_take(edges[2, level], high_index)),
        )
        high = jnp.where((rows == 1) | (rows == 2), 0.0, high)
        sums = []
        for corner in range(4):
            total = None
            for other in range(3):
                item = 3 * corner + other
                index = jnp.broadcast_to(ints[36 + item : 37 + item, :], (8, LANES)) + 4 * half
                value = row_take(corners[item, pair], index)
                total = value if total is None else total + value
            sums.append(total)
        low = jnp.where(rows == 0, sums[0], jnp.where(rows == 3, sums[1], low))
        high = jnp.where(rows == 7, sums[2], jnp.where(rows == 4, sums[3], high))
        pick[level, 0:8, :] = low
        pick[level, 8:16, :] = high


def group_rows(inverse, vertical):
    link0, link1 = vertical[7:8, :], vertical[15:16, :]
    up0 = link0 * inverse[0, 7, 0:1, :]
    up1 = link1 * inverse[1, 7, 0:1, :]
    down0 = link0 * inverse[0, 0, 7:8, :]
    down1 = link1 * inverse[1, 0, 7:8, :]
    response = inverse[0, 0, 0:1, :] + down0 * inverse[1, 0, 0:1, :] * up0
    return up1 * up0, response, down0 * down1


def group_response(load, inverse, vertical):
    link0, link1 = vertical[7:8, :], vertical[15:16, :]
    down0 = link0 * inverse[0, 0, 7:8, :]
    last0 = first0 = last1 = first1 = None
    for j in range(8):
        value0, value1 = load(j), load(8 + j)
        terms = (
            inverse[0, 7, j : j + 1, :] * value0,
            inverse[0, 0, j : j + 1, :] * value0,
            inverse[1, 7, j : j + 1, :] * value1,
            inverse[1, 0, j : j + 1, :] * value1,
        )
        if j == 0:
            last0, first0, last1, first1 = terms
        else:
            last0, first0, last1, first1 = (
                last0 + terms[0],
                first0 + terms[1],
                last1 + terms[2],
                first1 + terms[3],
            )
    carried = link0 * last0
    upward = link1 * (last1 + inverse[1, 7, 0:1, :] * carried)
    downward = first0 + down0 * (first1 + inverse[1, 0, 0:1, :] * carried)
    return upward, downward


def total_of(values):
    return jnp.sum(jnp.sum(values, axis=1, keepdims=True), axis=0, keepdims=True)


def begin_kernel(count, right_side, inverse, vertical, residual, message):
    tile = pl.program_id(0)
    lanes = lax.broadcasted_iota(jnp.int32, (NODES, LANES), 1)
    living = lanes + tile * LANES < count[0]

    for level in range(LEVELS):
        residual[level] = jnp.where(living, right_side[level], 0.0)
    upward, downward = group_response(lambda level: residual[level], inverse, vertical)
    message[0, 0:16, :] = upward
    message[0, 16:32, :] = downward
    coupling = group_rows(inverse, vertical)
    for row in range(3):
        message[0, 32 + row : 33 + row, :] = coupling[row]
    message[0, 35:40, :] = jnp.zeros((5, LANES), F32)


def scan_kernel(received, coupling, carried, dots):
    value = jnp.zeros((16, LANES), F32)
    for group in range(GROUPS):
        carried[group, 0:16, :] = value
        value = coupling[group, 0:1, :] * value + received[group, 0:16, :]
    value = jnp.zeros((16, LANES), F32)
    for group in reversed(range(GROUPS)):
        carried[group, 16:32, :] = value
        value = (
            received[group, 16:32, :]
            + coupling[group, 1:2, :] * carried[group, 0:16, :]
            + coupling[group, 2:3, :] * value
        )
    total = received[0, 32:33, :]
    for group in range(1, GROUPS):
        total = total + received[group, 32:33, :]
    dots[...] = jnp.broadcast_to(total, (16, LANES))


def solve_kernel(first, *refs):
    if first:
        count, residual_in, came, inverse, vertical = refs[:5]
        smoothed, product, tail, head, tables, parts = refs[5:]
        residual = residual_in
        state = came
    else:
        count, residual_in, image, came, state_in, dots, norm, inverse, vertical = refs[:9]
        residual, state, step, smoothed, product, tail, head, tables, parts = refs[9:]
        step_size = norm[0:1, :] / total_of(dots[...])
        for level in range(LEVELS):
            residual[level] = residual_in[level] - step_size * image[level]
        state[0] = state_in[0] - step_size * came[0]
        step[...] = jnp.broadcast_to(step_size, (8, LANES))
    tile = pl.program_id(0)
    rows, lanes = iotas()
    link0, link1 = vertical[7:8, :], vertical[15:16, :]
    below = state[0, 0:16, :]
    above = state[0, 16:32, :]

    def block_product(block, lifted):
        solved = []
        for i in range(8):
            total = inverse[block, i, 0:1, :] * lifted[0]
            for j in range(1, 8):
                total = total + inverse[block, i, j : j + 1, :] * lifted[j]
            solved.append(total)
        return solved

    values = [residual[level] for level in range(8)]
    lower = block_product(0, [values[0] + below] + values[1:])
    values = [residual[8 + level] for level in range(8)]
    upper = block_product(1, [values[0] + link0 * lower[7]] + values[1:])
    lift = link1 * above
    upper = [upper[i] + lift * inverse[1, i, 7:8, :] for i in range(8)]
    lift = link0 * upper[0]
    lower = [lower[i] + lift * inverse[0, i, 7:8, :] for i in range(8)]
    total = None
    for level, value in enumerate(lower + upper):
        smoothed[level] = value
        term = value * residual[level]
        total = term if total is None else total + term

    @pl.when(tile == 0)
    def clear():
        parts[...] = jnp.zeros((16, LANES), F32)
        tail[...] = jnp.zeros((25, 8, LANES), F32)
        head[...] = jnp.zeros((25, 8, LANES), F32)

    parts[...] += total

    @pl.when(tile == GROUPS - 1)
    def finish():
        product[...] = jnp.broadcast_to(jnp.sum(parts[...], axis=0, keepdims=True), (LANES, LANES))

    start = count[0] - LANES
    start_tile = lax.shift_right_logical(start, 7)
    offset = jnp.bitwise_and(start, LANES - 1)
    extra = start - 1
    extra_tile = lax.shift_right_logical(extra, 7)
    extra_lane = jnp.bitwise_and(extra, LANES - 1)
    in_tail = (tile == start_tile) | (tile == start_tile + 1)
    in_extra = tile == extra_tile

    def put(position, value):
        tables[position] = value

    @pl.when(in_tail | in_extra | (tile < 2))
    def build():
        store_tables(lambda level: smoothed[level], rows, put)

    @pl.when(in_tail)
    def fill_tail():
        index = jnp.bitwise_and(lanes + offset, LANES - 1)
        before_wrap = (lanes < LANES - offset).astype(jnp.int32)
        wanted = before_wrap == (tile == start_tile).astype(jnp.int32)
        for position in range(24):
            tail[position] = jnp.where(wanted, lane_take(tables[position], index), tail[position])

    @pl.when(in_extra)
    def fill_extra():
        index = jnp.zeros_like(lanes) + extra_lane
        packed = jnp.zeros((8, LANES), F32)
        for position in range(24):
            packed = jnp.where(lanes == position, lane_take(tables[position], index), packed)
        tail[24] = packed

    @pl.when(tile == 0)
    def fill_head():
        for position in range(24):
            head[position] = tables[position]

    @pl.when(tile == 1)
    def fill_head_extra():
        packed = jnp.zeros((8, LANES), F32)
        for position in range(24):
            packed = jnp.where(
                lanes == position, lane_take(tables[position], jnp.zeros_like(lanes)), packed
            )
        head[24] = packed


def split(values):
    high = values.astype(BF16)
    return high, (values - high.astype(F32)).astype(BF16)


def product3(table, values):
    high, low = split(values)
    result = jnp.dot(table[0], high, preferred_element_type=F32)
    result = result + jnp.dot(table[0], low, preferred_element_type=F32)
    return result + jnp.dot(table[1], high, preferred_element_type=F32)


def operate_kernel(
    helmholtz,
    counts,
    lists,
    field,
    ints,
    copies,
    metric,
    mass,
    vertical,
    below_row,
    state,
    forward,
    backward,
    applied,
    table,
    edges,
    corners,
    pick,
):
    tile = pl.program_id(0)
    rows, lanes = iotas()
    here = pl.ds(pl.multiple_of(tile * LANES, LANES), LANES)

    @pl.when(tile == 0)
    def build():
        def one(part, unused):
            there = pl.ds(pl.multiple_of(part * LANES, LANES), LANES)

            def put(position, value):
                table[position, :, there] = value

            store_tables(lambda level: field[level, :, there], rows, put)
            return unused

        lax.fori_loop(0, GROUPS, one, 0)

    gather_pick(table, 0, ints, counts, lists, 8, tile, edges, corners, pick)
    mixed, along_y, along_x = metric[1], metric[2], metric[0]
    for half in range(2):
        values = jnp.concatenate([field[8 * half + level, :, here] for level in range(8)], axis=0)
        gradients = product3(forward, values)
        flux_x = []
        flux_y = []
        for level in range(8):
            part_x = gradients[16 * level : 16 * level + 16]
            part_y = gradients[128 + 16 * level : 144 + 16 * level]
            flux_x.append(along_x * part_x + mixed * part_y)
            flux_y.append(mixed * part_x + along_y * part_y)
        stiff = product3(backward, jnp.concatenate(flux_x + flux_y, axis=0))
        for level in range(8):
            applied[8 * half + level] = stiff[16 * level : 16 * level + 16]
    twice = PENALTY * copies[...]
    flux = state[0, 0:16, :] + below_row[0:1, :] * field[0, :, here]
    for level in range(LEVELS):
        value = field[level, :, here]
        higher = field[level + 1, :, here] if level < LEVELS - 1 else state[0, 16:32, :]
        next_flux = vertical[level : level + 1, :] * (value - higher)
        applied[level] = (
            applied[level]
            + (helmholtz[level] * mass[...] + twice) * value
            + (next_flux - flux)
            - PENALTY * pick[level]
        )
        flux = next_flux


def image_kernel(first, *refs):
    if first:
        counts, lists, totals, applied, smoothed, ints, before, after, norms, inverse, vertical = refs[:11]
        refs = refs[11:]
    else:
        counts, lists, totals, applied, smoothed, ints, before, after, norms, inverse, vertical = refs[:11]
        norm_in, direction_in, image_in = refs[11:14]
        refs = refs[14:]
    direction, image, message, norm, table, edges, corners, pick, parts = refs
    tile = pl.program_id(0)
    rows, lanes = iotas()
    new = total_of(norms[...])
    norm[...] = jnp.broadcast_to(new, (8, LANES))

    @pl.when(tile == 0)
    def build():
        parts[...] = jnp.zeros((16, LANES), F32)
        for position in range(24):
            index = jnp.full((8, LANES), position, jnp.int32)
            table[position, :, 0:LANES] = before[position]
            table[position, :, LANES : 2 * LANES] = after[position]
            table[position, :, 2 * LANES : 3 * LANES] = jnp.where(
                lanes == 0, lane_take(before[24], index), lane_take(after[24], index)
            )

    pick[...] = jnp.zeros((LEVELS, NODES, LANES), F32)

    @pl.when(totals[tile] > 0)
    def reach():
        gather_pick(table, 8, ints, counts, lists, 3, tile, edges, corners, pick)

    if not first:
        ratio = new / norm_in[0:1, :]
    total = None
    for level in range(LEVELS):
        value = smoothed[level]
        result = applied[level] - PENALTY * pick[level]
        if not first:
            value = value + ratio * direction_in[level]
            result = result + ratio * image_in[level]
        direction[level] = value
        image[level] = result
        term = value * result
        total = term if total is None else total + term
    parts[...] += total
    upward, downward = group_response(lambda level: image[level], inverse, vertical)
    message[tile, 0:16, :] = upward
    message[tile, 16:32, :] = downward

    @pl.when(tile == GROUPS - 1)
    def finish():
        dot = jnp.sum(parts[...], axis=0, keepdims=True)
        for target in range(GROUPS):
            message[target, 32:33, :] = dot
            message[target, 33:40, :] = jnp.zeros((7, LANES), F32)


def field_spec():
    return pl.BlockSpec((LEVELS, NODES, LANES), lambda t: (0, 0, t))


def row_spec(rows):
    return pl.BlockSpec((rows, LANES), lambda t: (0, t))


def whole(*shape):
    return pl.BlockSpec(shape, lambda t: (0,) * len(shape))


def tile_spec(rows):
    return pl.BlockSpec((1, rows, LANES), lambda t: (t, 0, 0))


def inverse_spec():
    return pl.BlockSpec((2, 8, 8, LANES), lambda t: (0, 0, 0, t))


def scalars():
    return pl.BlockSpec(memory_space=pltpu.SMEM)


def struct(*shape):
    return jax.ShapeDtypeStruct(shape, F32)


def call(kernel, name, in_specs, out_specs, out_shape, scratch, cost, args):
    return pl.pallas_call(
        kernel,
        grid=(GROUPS,),
        in_specs=in_specs,
        out_specs=out_specs,
        out_shape=out_shape,
        scratch_shapes=scratch,
        name=name,
        compiler_params=pltpu.CompilerParams(
            dimension_semantics=("arbitrary",), vmem_limit_bytes=VMEM_BYTES
        ),
        cost_estimate=pl.CostEstimate(flops=cost, bytes_accessed=6 << 20, transcendentals=0),
    )(*args)


FIELD = (LEVELS, NODES, 1024)
PICK_SCRATCH = [
    ((4, LEVELS, 8, LANES), F32),
    ((12, 8, 8, LANES), F32),
    ((LEVELS, NODES, LANES), F32),
]


def vmem(shapes):
    return [pltpu.VMEM(shape, dtype) for shape, dtype in shapes]


def neighbour_lists(source, first_tile, tile_count):
    holder = (source // LANES).reshape(16, 8, LANES)
    tiles = first_tile + jnp.arange(tile_count, dtype=jnp.int32)
    used = jnp.any(holder[:, :, None, :] == tiles[None, None, :, None], axis=3)
    place = jnp.cumsum(used.astype(jnp.int32), axis=2) - 1
    slots = jnp.arange(tile_count, dtype=jnp.int32)
    chosen = used[:, :, :, None] & (place[:, :, :, None] == slots)
    lists = jnp.sum(jnp.where(chosen, tiles[None, None, :, None], 0), axis=2)
    counts = jnp.sum(used.astype(jnp.int32), axis=2)
    return counts, lists.astype(jnp.int32)


def neighbour_tables(edge_neighbour, edge_flip, corner_neighbour, count_before, position):
    slot_count = edge_neighbour.shape[0]

    def locate(element):
        holder = element // slot_count
        within = element % slot_count
        earlier = within - (count_before - BORDER)
        earlier = jnp.where(earlier == 0, 10 * LANES, 8 * LANES + earlier - 1)
        later = jnp.where(within < LANES, 9 * LANES + within, 10 * LANES + 1)
        return jnp.where(holder == position, within, jnp.where(holder < position, earlier, later))

    edges = jnp.transpose(edge_neighbour)
    flips = jnp.transpose(edge_flip)
    corners = jnp.transpose(corner_neighbour, (1, 2, 0)).reshape(12, slot_count)
    everything = jnp.concatenate([edges, corners], axis=0)
    present = everything >= 0
    target = jnp.where(present, everything, 0)
    source = jnp.where(present, locate(target // 4), ABSENT)
    side = target % 4
    straight = 2 * side[:4] + jnp.where(flips == 1, 1, 0)
    swapped = 2 * side[:4] + jnp.where(flips == 1, 0, 1)
    none = jnp.zeros_like(straight[0])
    low = [none, straight[0], swapped[0], none, straight[3], none, none, straight[1]]
    high = [swapped[3], none, none, swapped[1], none, straight[2], swapped[2], none]
    ints = jnp.concatenate([source, jnp.stack(low), jnp.stack(high), side], axis=0).astype(jnp.int32)
    on = present.astype(F32)
    shared = jnp.sum(on[4:].reshape(4, 3, slot_count), axis=1)
    nothing = jnp.zeros_like(shared[0])
    copies = jnp.stack(
        [
            shared[0], on[0], on[0], shared[1], on[3], nothing, nothing, on[1],
            on[3], nothing, nothing, on[1], shared[3], on[2], on[2], shared[2],
        ]
    )
    return source, ints, copies


def body(
    right_side,
    metric,
    mass_weight,
    helmholtz,
    vertical,
    block_inverse,
    edge_neighbour,
    edge_flip,
    corner_neighbour,
    element_count,
):
    peers = lax.axis_size("elem")
    groups = lax.axis_size("lev")
    position = lax.axis_index("elem")
    upward_elem = [(i, i + 1) for i in range(peers - 1)]
    downward_elem = [(i + 1, i) for i in range(peers - 1)]
    upward_lev = [(i, i + 1) for i in range(groups - 1)]

    residual, message = call(
        begin_kernel,
        "begin",
        [scalars(), field_spec(), inverse_spec(), row_spec(16)],
        [field_spec(), tile_spec(40)],
        [struct(*FIELD), struct(8, 40, LANES)],
        [],
        1 << 22,
        (element_count, right_side, block_inverse, vertical),
    )
    received = lax.all_to_all(message, "lev", split_axis=0, concat_axis=0, tiled=True)
    coupling = received[:, 32:40, :]

    def scan_groups(received):
        return pl.pallas_call(
            scan_kernel,
            out_shape=[struct(8, 32, LANES), struct(16, LANES)],
            name="scan",
            cost_estimate=pl.CostEstimate(flops=1 << 16, bytes_accessed=1 << 18, transcendentals=0),
        )(received, coupling)

    carried, unused = scan_groups(received)
    came = lax.all_to_all(carried, "lev", split_axis=0, concat_axis=0, tiled=True)

    count_before = lax.ppermute(element_count, "elem", upward_elem)[0]
    edge_rows = jnp.stack([vertical[15], block_inverse[1, 7, 7]])
    rows_below = lax.ppermute(edge_rows, "lev", upward_lev)
    below_row = (rows_below[0] * (rows_below[0] * rows_below[1] - 1.0))[None]
    source, ints, copies = neighbour_tables(
        edge_neighbour, edge_flip, corner_neighbour, count_before, position
    )
    own_counts, own_lists = neighbour_lists(source, 0, 8)
    far_counts, far_lists = neighbour_lists(source, 8, 3)
    far_totals = jnp.sum(far_counts, axis=0)
    own_counts, own_lists = own_counts.reshape(-1), own_lists.reshape(-1)
    far_counts, far_lists = far_counts.reshape(-1), far_lists.reshape(-1)
    forward, backward = stacked_tables()

    solve_scratch = vmem([((24, 8, LANES), F32), ((16, LANES), F32)])
    solve_outs = ([field_spec(), whole(LANES, LANES), whole(25, 8, LANES), whole(25, 8, LANES)],
                  [struct(*FIELD), struct(LANES, LANES), struct(25, 8, LANES), struct(25, 8, LANES)])
    smoothed, product, tail, head = call(
        lambda *refs: solve_kernel(True, *refs),
        "solve_first",
        [scalars(), field_spec(), tile_spec(32), inverse_spec(), row_spec(16)],
        *solve_outs,
        solve_scratch,
        1 << 22,
        (element_count, residual, came, block_inverse, vertical),
    )
    state = came
    solution = direction = image = norm = None
    for iteration in range(ITERATIONS):
        norms = lax.all_to_all(product, ("elem", "lev"), split_axis=0, concat_axis=0, tiled=True)
        before = lax.ppermute(tail, "elem", upward_elem)
        after = lax.ppermute(head, "elem", downward_elem)
        applied = call(
            operate_kernel,
            "operate",
            [
                scalars(), scalars(), scalars(), whole(*FIELD), row_spec(48), row_spec(16),
                pl.BlockSpec((3, NODES, LANES), lambda t: (0, 0, t)), row_spec(16), row_spec(16),
                row_spec(1), tile_spec(32), whole(2, 256, 128), whole(2, 128, 256),
            ],
            field_spec(),
            struct(*FIELD),
            vmem([((24, 8, 1024), F32)] + PICK_SCRATCH),
            1 << 30,
            (
                helmholtz, own_counts, own_lists, smoothed, ints, copies, metric, mass_weight,
                vertical, below_row, state, forward, backward,
            ),
        )
        first = iteration == 0
        args = [
            far_counts, far_lists, far_totals, applied, smoothed, ints, before, after, norms,
            block_inverse, vertical,
        ]
        specs = [
            scalars(), scalars(), scalars(), field_spec(), field_spec(), row_spec(48),
            whole(25, 8, LANES), whole(25, 8, LANES), whole(LANES, LANES), inverse_spec(), row_spec(16),
        ]
        if not first:
            args += [norm, direction, image]
            specs += [whole(8, LANES), field_spec(), field_spec()]
        direction, image, message, norm = call(
            lambda *refs, first=first: image_kernel(first, *refs),
            "image_first" if first else "image",
            specs,
            [field_spec(), field_spec(), whole(8, 40, LANES), whole(8, LANES)],
            [struct(*FIELD), struct(*FIELD), struct(8, 40, LANES), struct(8, LANES)],
            vmem([((24, 8, 3 * LANES), F32)] + PICK_SCRATCH + [((16, LANES), F32)]),
            1 << 22,
            args,
        )
        received = lax.all_to_all(message, "lev", split_axis=0, concat_axis=0, tiled=True)
        carried, dots = scan_groups(received)
        came = lax.all_to_all(carried, "lev", split_axis=0, concat_axis=0, tiled=True)
        dots = lax.all_to_all(dots, "elem", split_axis=0, concat_axis=0, tiled=True)
        residual, state, step, smoothed, product, tail, head = call(
            lambda *refs: solve_kernel(False, *refs),
            "solve",
            [
                scalars(), field_spec(), field_spec(), tile_spec(32), tile_spec(32), whole(16, LANES),
                whole(8, LANES), inverse_spec(), row_spec(16),
            ],
            [field_spec(), tile_spec(32), whole(8, LANES)] + solve_outs[0],
            [struct(*FIELD), struct(8, 32, LANES), struct(8, LANES)] + solve_outs[1],
            solve_scratch,
            1 << 22,
            (element_count, residual, image, came, state, dots, norm, block_inverse, vertical),
        )
        moved = step[0, 0] * direction
        solution = moved if first else solution + moved
    norms = lax.all_to_all(product, ("elem", "lev"), split_axis=0, concat_axis=0, tiled=True)
    direction = smoothed + jnp.sum(norms) / norm[0, 0] * direction
    return (solution, residual, direction)


def solution(mesh):
    in_specs = (
        P("lev", None, "elem"),
        P(None, None, "elem"),
        P(None, "elem"),
        P("lev"),
        P("lev", "elem"),
        P("lev", None, None, "elem"),
        P("elem", None),
        P("elem", None),
        P("elem", None, None),
        P("elem"),
    )
    out_specs = (P("lev", None, "elem"), P("lev", None, "elem"), P("lev", None, "elem"))
    return jax.shard_map(body, mesh=mesh, in_specs=in_specs, out_specs=out_specs, check_vma=False)
```

```python
import math

import jax
import jax.numpy as jnp
import numpy as np
from jax import lax
from jax.experimental import pallas as pl
from jax.experimental.pallas import tpu as pltpu
from jax.sharding import PartitionSpec as P

COLUMNS = 128
ITERATIONS = 3
BORDER = COLUMNS + 1
LANES = 128
LEVELS = 16
NODES = 16
GROUPS = 8
PENALTY = 2.0
ABSENT = 15 * LANES
VMEM_BYTES = 12 * 1024 * 1024
SMALL_VMEM_BYTES = 4 * 1024 * 1024
F32 = jnp.float32
BF16 = jnp.bfloat16


def gradient_table():
    root = 1.0 / math.sqrt(5.0)
    points = [-1.0, -root, root, 1.0]
    legendre = [0.5 * (5.0 * p * p * p - 3.0 * p) for p in points]
    matrix = [[0.0 for col in range(4)] for row in range(4)]
    for row in range(4):
        for col in range(4):
            if row != col:
                matrix[row][col] = legendre[row] / (legendre[col] * (points[row] - points[col]))
    matrix[0][0] = -3.0
    matrix[3][3] = 3.0
    derivative = np.array(matrix)
    return np.kron(np.eye(4), derivative), np.kron(derivative, np.eye(4))


def stacked_tables():
    along_x, along_y = gradient_table()
    table = np.concatenate([np.kron(np.eye(8), along_x), np.kron(np.eye(8), along_y)], axis=0)
    table = jnp.asarray(table, F32)
    high = table.astype(BF16)
    low = (table - high.astype(F32)).astype(BF16)
    return jnp.stack([high, low]), jnp.stack([high.T, low.T])


def lane_take(values, index):
    return jnp.take_along_axis(values, index, axis=1, mode="promise_in_bounds")


def row_take(values, index):
    return jnp.take_along_axis(values, index, axis=0, mode="promise_in_bounds")


def iotas():
    rows = lax.broadcasted_iota(jnp.int32, (8, LANES), 0)
    lanes = lax.broadcasted_iota(jnp.int32, (8, LANES), 1)
    return rows, lanes


def by_row(rows, values):
    index = jnp.zeros_like(rows)
    for row, value in enumerate(values):
        if value:
            index = jnp.where(rows == row, value, index)
    return index


def edge_table(low, high, rows):
    from_low = row_take(low, by_row(rows, [1, 2, 7, 0, 0, 0, 4, 0]))
    from_high = row_take(high, by_row(rows, [0, 0, 0, 3, 5, 6, 0, 0]))
    use_low = (rows < 3) | (rows == 6)
    return jnp.where(use_low, from_low, from_high)


def corner_table(low, high, low_next, high_next, rows):
    index_low = by_row(rows, [0, 3, 0, 0, 0, 3, 0, 0])
    index_high = by_row(rows, [0, 0, 7, 4, 0, 0, 7, 4])
    first = jnp.where(rows < 2, row_take(low, index_low), row_take(high, index_high))
    second = jnp.where(rows < 6, row_take(low_next, index_low), row_take(high_next, index_high))
    return jnp.where(rows < 4, first, second)


def store_tables(load, rows, put):
    for pair in range(LEVELS // 2):
        even = load(2 * pair)
        odd = load(2 * pair + 1)
        put(2 * pair, edge_table(even[:8], even[8:], rows))
        put(2 * pair + 1, edge_table(odd[:8], odd[8:], rows))
        put(LEVELS + pair, corner_table(even[:8], even[8:], odd[:8], odd[8:], rows))


def gather_pick(table, first_tile, ints, counts, lists, per_list, tile, edges, corners, pick):
    rows, lanes = iotas()
    edges[...] = jnp.zeros(edges.shape, F32)
    corners[...] = jnp.zeros(corners.shape, F32)

    def step(turn, unused):
        which = lists[tile * per_list + turn]
        column = pl.multiple_of((which - first_tile) * LANES, LANES)
        values = [table[member, :, pl.ds(column, LANES)] for member in range(LEVELS + 8)]
        for side in range(4):
            source = jnp.broadcast_to(ints[side : side + 1, :], (8, LANES))
            lane = jnp.bitwise_and(source, LANES - 1)
            hit = lax.shift_right_logical(source, 7) == which
            for place in range(LEVELS):
                edges[side, place] = jnp.where(
                    hit, lane_take(values[place], lane), edges[side, place]
                )
        for corner in range(4):
            sums = [corners[corner, place] for place in range(8)]
            for other in range(3):
                item = 4 + 3 * corner + other
                source = jnp.broadcast_to(ints[item : item + 1, :], (8, LANES))
                node = jnp.broadcast_to(ints[32 + item : 33 + item, :], (8, LANES))
                lane = jnp.bitwise_and(source, LANES - 1)
                hit = (lax.shift_right_logical(source, 7) == which) & (
                    jnp.bitwise_and(rows, 3) == node
                )
                for place in range(8):
                    sums[place] = sums[place] + jnp.where(
                        hit, lane_take(values[LEVELS + place], lane), 0.0
                    )
            for place in range(8):
                corners[corner, place] = sums[place]
        return unused

    lax.fori_loop(0, counts[tile], step, 0)
    low_index = ints[16:24, :]
    high_index = ints[24:32, :]
    next_row = jnp.bitwise_and(rows, 4) + jnp.bitwise_and(rows + 1, 3)
    next_pair = jnp.bitwise_and(rows, 4) + jnp.bitwise_and(rows + 2, 3)
    other_half = jnp.bitwise_xor(rows, 4)
    for pair in range(LEVELS // 2):
        sums = []
        for corner in range(4):
            total = corners[corner, pair]
            total = total + row_take(total, next_row)
            total = total + row_take(total, next_pair)
            sums.append((total, row_take(total, other_half)))
        for half in range(2):
            level = 2 * pair + half
            low = jnp.where(
                (rows == 1) | (rows == 2),
                row_take(edges[0, level], low_index),
                jnp.where(
                    rows == 7,
                    row_take(edges[1, level], low_index),
                    row_take(edges[3, level], low_index),
                ),
            )
            low = jnp.where((rows == 5) | (rows == 6), 0.0, low)
            high = jnp.where(
                rows == 3,
                row_take(edges[1, level], high_index),
                jnp.where(
                    rows == 0,
                    row_take(edges[3, level], high_index),
                    row_take(edges[2, level], high_index),
                ),
            )
            high = jnp.where((rows == 1) | (rows == 2), 0.0, high)
            low = jnp.where(rows == 0, sums[0][half], jnp.where(rows == 3, sums[1][half], low))
            high = jnp.where(rows == 7, sums[2][1 - half], jnp.where(rows == 4, sums[3][1 - half], high))
            pick[level, 0:8, :] = low
            pick[level, 8:16, :] = high


def group_rows(inverse, vertical):
    link0, link1 = vertical[7:8, :], vertical[15:16, :]
    up0 = link0 * inverse[0, 7, 0:1, :]
    up1 = link1 * inverse[1, 7, 0:1, :]
    down0 = link0 * inverse[0, 0, 7:8, :]
    down1 = link1 * inverse[1, 0, 7:8, :]
    response = inverse[0, 0, 0:1, :] + down0 * inverse[1, 0, 0:1, :] * up0
    return up1 * up0, response, down0 * down1


def group_response(load, inverse, vertical):
    link0, link1 = vertical[7:8, :], vertical[15:16, :]
    down0 = link0 * inverse[0, 0, 7:8, :]
    last0 = first0 = last1 = first1 = None
    for j in range(8):
        value0, value1 = load(j), load(8 + j)
        terms = (
            inverse[0, 7, j : j + 1, :] * value0,
            inverse[0, 0, j : j + 1, :] * value0,
            inverse[1, 7, j : j + 1, :] * value1,
            inverse[1, 0, j : j + 1, :] * value1,
        )
        if j == 0:
            last0, first0, last1, first1 = terms
        else:
            last0, first0, last1, first1 = (
                last0 + terms[0],
                first0 + terms[1],
                last1 + terms[2],
                first1 + terms[3],
            )
    carried = link0 * last0
    upward = link1 * (last1 + inverse[1, 7, 0:1, :] * carried)
    downward = first0 + down0 * (first1 + inverse[1, 0, 0:1, :] * carried)
    return upward, downward


def total_of(values):
    return jnp.sum(jnp.sum(values, axis=1, keepdims=True), axis=0, keepdims=True)


def begin_kernel(count, right_side, inverse, vertical, residual, message):
    tile = pl.program_id(0)
    lanes = lax.broadcasted_iota(jnp.int32, (NODES, LANES), 1)
    living = lanes + tile * LANES < count[0]

    for level in range(LEVELS):
        residual[level] = jnp.where(living, right_side[level], 0.0)
    upward, downward = group_response(lambda level: residual[level], inverse, vertical)
    message[0, 0:16, :] = upward
    message[0, 16:32, :] = downward
    coupling = group_rows(inverse, vertical)
    for row in range(3):
        message[0, 32 + row : 33 + row, :] = coupling[row]
    link = vertical[15:16, :]
    message[0, 35:36, :] = link * (link * inverse[1, 7, 7:8, :] - 1.0)
    message[0, 36:40, :] = jnp.zeros((4, LANES), F32)


def scan_groups(received, coupling, carried):
    value = jnp.zeros((16, LANES), F32)
    for group in range(GROUPS):
        carried[group, 0:16, :] = value
        value = coupling[group, 32:33, :] * value + received[group, 0:16, :]
    value = jnp.zeros((16, LANES), F32)
    for group in reversed(range(GROUPS)):
        carried[group, 16:32, :] = value
        value = (
            received[group, 16:32, :]
            + coupling[group, 33:34, :] * carried[group, 0:16, :]
            + coupling[group, 34:35, :] * value
        )


def scan_first_kernel(received, carried):
    scan_groups(received, received, carried)
    for group in range(GROUPS):
        below = received[group - 1, 35:36, :] if group else jnp.zeros((1, LANES), F32)
        carried[group, 32:40, :] = jnp.broadcast_to(below, (8, LANES))


def scan_kernel(received, coupling, carried, dots):
    scan_groups(received, coupling, carried)
    total = received[0, 32:40, :]
    for group in range(1, GROUPS):
        total = total + received[group, 32:40, :]
    dots[...] = total


def solve_kernel(stage, last, *refs):
    refs = list(refs)

    def take(count):
        taken = refs[:count]
        del refs[:count]
        return taken

    count, inverse, vertical, residual_in, came = take(5)
    if stage:
        smoothed_in, applied, state_in, dots = take(4)
    if stage == 2:
        solution_in, direction_in, image_in, flow_in, scalars_in = take(5)
    if stage:
        solution, residual, direction, scalars_out = take(4)
        if not last:
            image, flow, state = take(3)
    else:
        residual, state = residual_in, came
    smoothed, product = take(2)
    if not last:
        tail, head, tables = take(3)
    (parts,) = take(1)
    tile = pl.program_id(0)
    rows, lanes = iotas()

    if stage:
        norm = jnp.sum(dots[0:1, :], axis=1, keepdims=True)
        curvature = jnp.sum(dots[1:2, :], axis=1, keepdims=True)
        if stage == 2:
            cross = jnp.sum(dots[2:3, :], axis=1, keepdims=True)
            ratio = norm / scalars_in[0:1, 0:1]
            curvature = curvature + ratio * cross + ratio * ratio * scalars_in[1:2, 0:1]
        step_size = norm / curvature
        scalars_out[0:1, :] = jnp.broadcast_to(norm, (1, LANES))
        scalars_out[1:2, :] = jnp.broadcast_to(curvature, (1, LANES))
        scalars_out[2:8, :] = jnp.zeros((6, LANES), F32)
        for level in range(LEVELS):
            value = smoothed_in[level]
            result = applied[level]
            if stage == 2:
                value = value + ratio * direction_in[level]
                result = result + ratio * image_in[level]
                solution[level] = solution_in[level] + step_size * value
            else:
                solution[level] = step_size * value
            direction[level] = value
            if not last:
                image[level] = result
            residual[level] = residual_in[level] - step_size * result
        change = came[0, 0:32, :]
        if stage == 2:
            change = change + ratio * flow_in[0]
        incoming = state_in[0, 0:32, :] - step_size * change
        if not last:
            flow[0] = change
            state[0] = incoming
    else:
        incoming = came[0, 0:32, :]
    link0, link1 = vertical[7:8, :], vertical[15:16, :]
    below = incoming[0:16]
    above = incoming[16:32]

    def block_product(block, lifted):
        solved = []
        for i in range(8):
            total = inverse[block, i, 0:1, :] * lifted[0]
            for j in range(1, 8):
                total = total + inverse[block, i, j : j + 1, :] * lifted[j]
            solved.append(total)
        return solved

    values = [residual[level] for level in range(8)]
    lower = block_product(0, [values[0] + below] + values[1:])
    values = [residual[8 + level] for level in range(8)]
    upper = block_product(1, [values[0] + link0 * lower[7]] + values[1:])
    lift = link1 * above
    upper = [upper[i] + lift * inverse[1, i, 7:8, :] for i in range(8)]
    lift = link0 * upper[0]
    lower = [lower[i] + lift * inverse[0, i, 7:8, :] for i in range(8)]
    total = None
    for level, value in enumerate(lower + upper):
        smoothed[level] = value
        term = value * residual[level]
        total = term if total is None else total + term

    @pl.when(tile == 0)
    def clear():
        parts[...] = jnp.zeros((16, LANES), F32)

    parts[...] += total

    @pl.when(tile == GROUPS - 1)
    def finish():
        product[...] = jnp.broadcast_to(jnp.sum(parts[...], axis=0, keepdims=True), product.shape)

    if last:
        return

    @pl.when(tile == 0)
    def clear_tail():
        tail[...] = jnp.zeros((25, 8, LANES), F32)
        head[...] = jnp.zeros((25, 8, LANES), F32)

    start = count[0] - LANES
    start_tile = lax.shift_right_logical(start, 7)
    offset = jnp.bitwise_and(start, LANES - 1)
    extra = start - 1
    extra_tile = lax.shift_right_logical(extra, 7)
    extra_lane = jnp.bitwise_and(extra, LANES - 1)
    in_tail = (tile == start_tile) | (tile == start_tile + 1)
    in_extra = tile == extra_tile

    def put(position, value):
        tables[position] = value

    @pl.when(in_tail | in_extra | (tile < 2))
    def build():
        store_tables(lambda level: smoothed[level], rows, put)

    @pl.when(in_tail)
    def fill_tail():
        index = jnp.bitwise_and(lanes + offset, LANES - 1)
        before_wrap = (lanes < LANES - offset).astype(jnp.int32)
        wanted = before_wrap == (tile == start_tile).astype(jnp.int32)
        for position in range(24):
            tail[position] = jnp.where(wanted, lane_take(tables[position], index), tail[position])

    @pl.when(in_extra)
    def fill_extra():
        index = jnp.zeros_like(lanes) + extra_lane
        packed = jnp.zeros((8, LANES), F32)
        for position in range(24):
            packed = jnp.where(lanes == position, lane_take(tables[position], index), packed)
        tail[24] = packed

    @pl.when(tile == 0)
    def fill_head():
        for position in range(24):
            head[position] = tables[position]

    @pl.when(tile == 1)
    def fill_head_extra():
        packed = jnp.zeros((8, LANES), F32)
        for position in range(24):
            packed = jnp.where(
                lanes == position, lane_take(tables[position], jnp.zeros_like(lanes)), packed
            )
        head[24] = packed


def finish_kernel(norms, scalars_in, smoothed, direction_in, direction):
    ratio = total_of(norms[...]) / scalars_in[0:1, 0:1]
    for level in range(LEVELS):
        direction[level] = smoothed[level] + ratio * direction_in[level]


def split(values):
    high = values.astype(BF16)
    return high, (values - high.astype(F32)).astype(BF16)


def product3(table, values):
    high, low = split(values)
    result = jnp.dot(table[0], high, preferred_element_type=F32)
    result = result + jnp.dot(table[0], low, preferred_element_type=F32)
    return result + jnp.dot(table[1], high, preferred_element_type=F32)


def operate_kernel(
    helmholtz,
    counts,
    lists,
    field,
    ints,
    copies,
    metric,
    mass,
    vertical,
    below_row,
    state,
    forward,
    backward,
    applied,
    table,
    edges,
    corners,
    pick,
):
    tile = pl.program_id(0)
    rows, lanes = iotas()
    here = pl.ds(pl.multiple_of(tile * LANES, LANES), LANES)

    @pl.when(tile == 0)
    def build():
        def one(part, unused):
            there = pl.ds(pl.multiple_of(part * LANES, LANES), LANES)

            def put(position, value):
                table[position, :, there] = value

            store_tables(lambda level: field[level, :, there], rows, put)
            return unused

        lax.fori_loop(0, GROUPS, one, 0)

    gather_pick(table, 0, ints, counts, lists, 8, tile, edges, corners, pick)
    mixed, along_y, along_x = metric[1], metric[2], metric[0]
    for half in range(2):
        values = jnp.concatenate([field[8 * half + level, :, here] for level in range(8)], axis=0)
        gradients = product3(forward, values)
        flux_x = []
        flux_y = []
        for level in range(8):
            part_x = gradients[16 * level : 16 * level + 16]
            part_y = gradients[128 + 16 * level : 144 + 16 * level]
            flux_x.append(along_x * part_x + mixed * part_y)
            flux_y.append(mixed * part_x + along_y * part_y)
        stiff = product3(backward, jnp.concatenate(flux_x + flux_y, axis=0))
        for level in range(8):
            applied[8 * half + level] = stiff[16 * level : 16 * level + 16]
    twice = PENALTY * copies[...]
    flux = state[0, 0:16, :] + below_row[0, 32:33, :] * field[0, :, here]
    for level in range(LEVELS):
        value = field[level, :, here]
        higher = field[level + 1, :, here] if level < LEVELS - 1 else state[0, 16:32, :]
        next_flux = vertical[level : level + 1, :] * (value - higher)
        applied[level] = (
            applied[level]
            + (helmholtz[level] * mass[...] + twice) * value
            + (next_flux - flux)
            - PENALTY * pick[level]
        )
        flux = next_flux


def image_kernel(first, *refs):
    counts, lists, applied, smoothed, ints, before, after, product, inverse, vertical = refs[:10]
    refs = refs[10:]
    if not first:
        direction, previous = refs[:2]
        refs = refs[2:]
    image, message, table, edges, corners, pick, parts, crosses = refs
    tile = pl.program_id(0)
    rows, lanes = iotas()

    @pl.when(tile == 0)
    def build():
        parts[...] = jnp.zeros((16, LANES), F32)
        crosses[...] = jnp.zeros((16, LANES), F32)
        for position in range(24):
            index = jnp.full((8, LANES), position, jnp.int32)
            table[position, :, 0:LANES] = before[position]
            table[position, :, LANES : 2 * LANES] = after[position]
            table[position, :, 2 * LANES : 3 * LANES] = jnp.where(
                lanes == 0, lane_take(before[24], index), lane_take(after[24], index)
            )

    pick[...] = jnp.zeros((LEVELS, NODES, LANES), F32)

    @pl.when(counts[tile] > 0)
    def reach():
        gather_pick(table, 8, ints, counts, lists, 3, tile, edges, corners, pick)

    total = cross = None
    for level in range(LEVELS):
        value = smoothed[level]
        result = applied[level] - PENALTY * pick[level]
        image[level] = result
        term = value * result
        total = term if total is None else total + term
        if not first:
            term = value * previous[level] + direction[level] * result
            cross = term if cross is None else cross + term
    parts[...] += total
    if not first:
        crosses[...] += cross
    upward, downward = group_response(lambda level: image[level], inverse, vertical)
    message[tile, 0:16, :] = upward
    message[tile, 16:32, :] = downward

    @pl.when(tile == GROUPS - 1)
    def finish():
        curvature = jnp.sum(parts[...], axis=0, keepdims=True)
        mixed = jnp.sum(crosses[...], axis=0, keepdims=True)
        for target in range(GROUPS):
            message[target, 32:33, :] = product[0:1, :]
            message[target, 33:34, :] = curvature
            message[target, 34:35, :] = mixed
            message[target, 35:40, :] = jnp.zeros((5, LANES), F32)


def field_spec():
    return pl.BlockSpec((LEVELS, NODES, LANES), lambda t: (0, 0, t))


def row_spec(rows):
    return pl.BlockSpec((rows, LANES), lambda t: (0, t))


def whole(*shape):
    return pl.BlockSpec(shape, lambda t: (0,) * len(shape))


def tile_spec(rows):
    return pl.BlockSpec((1, rows, LANES), lambda t: (t, 0, 0))


def inverse_spec():
    return pl.BlockSpec((2, 8, 8, LANES), lambda t: (0, 0, 0, t))


def scalars():
    return pl.BlockSpec(memory_space=pltpu.SMEM)


def struct(*shape):
    return jax.ShapeDtypeStruct(shape, F32)


def call(kernel, name, in_specs, out_specs, out_shape, scratch, cost, args):
    return pl.pallas_call(
        kernel,
        grid=(GROUPS,),
        in_specs=in_specs,
        out_specs=out_specs,
        out_shape=out_shape,
        scratch_shapes=scratch,
        name=name,
        compiler_params=pltpu.CompilerParams(
            dimension_semantics=("arbitrary",), vmem_limit_bytes=VMEM_BYTES
        ),
        cost_estimate=pl.CostEstimate(flops=cost, bytes_accessed=6 << 20, transcendentals=0),
    )(*args)


FIELD = (LEVELS, NODES, 1024)
PICK_SCRATCH = [
    ((4, LEVELS, 8, LANES), F32),
    ((4, 8, 8, LANES), F32),
    ((LEVELS, NODES, LANES), F32),
]


def vmem(shapes):
    return [pltpu.VMEM(shape, dtype) for shape, dtype in shapes]


def neighbour_lists(source, first_tile, tile_count):
    holder = (source // LANES).reshape(16, 8, LANES)
    tiles = first_tile + jnp.arange(tile_count, dtype=jnp.int32)
    used = jnp.any(holder[:, :, None, :] == tiles[None, None, :, None], axis=(0, 3))
    slots = jnp.arange(tile_count, dtype=jnp.int32)
    earlier = used[:, None, :] & (slots[None, None, :] < slots[None, :, None])
    place = jnp.sum(earlier.astype(jnp.int32), axis=2)
    chosen = used[:, :, None] & (place[:, :, None] == slots)
    lists = jnp.sum(jnp.where(chosen, tiles[None, :, None], 0), axis=1)
    return jnp.sum(used.astype(jnp.int32), axis=1), lists.astype(jnp.int32).reshape(-1)


def sum_over_elem(value, peers):
    side = math.isqrt(peers)
    for inner in (True, False):
        total = value
        for shift in range(1, side):
            pairs = []
            for i in range(peers):
                outer, within = i // side, i % side
                if inner:
                    pairs.append((i, outer * side + (within + shift) % side))
                else:
                    pairs.append((i, (outer + shift) % side * side + within))
            total = total + lax.ppermute(value, "elem", pairs)
        value = total
    return value


def neighbour_tables(edge_neighbour, edge_flip, corner_neighbour, count_before, position):
    slot_count = edge_neighbour.shape[0]

    def locate(element):
        holder = element // slot_count
        within = element % slot_count
        earlier = within - (count_before - BORDER)
        earlier = jnp.where(earlier == 0, 10 * LANES, 8 * LANES + earlier - 1)
        later = jnp.where(within < LANES, 9 * LANES + within, 10 * LANES + 1)
        return jnp.where(holder == position, within, jnp.where(holder < position, earlier, later))

    edges = jnp.transpose(edge_neighbour)
    flips = jnp.transpose(edge_flip)
    corners = jnp.transpose(corner_neighbour, (1, 2, 0)).reshape(12, slot_count)
    everything = jnp.concatenate([edges, corners], axis=0)
    present = everything >= 0
    target = jnp.where(present, everything, 0)
    source = jnp.where(present, locate(target // 4), ABSENT)
    side = target % 4
    straight = 2 * side[:4] + jnp.where(flips == 1, 1, 0)
    swapped = 2 * side[:4] + jnp.where(flips == 1, 0, 1)
    none = jnp.zeros_like(straight[0])
    low = [none, straight[0], swapped[0], none, straight[3], none, none, straight[1]]
    high = [swapped[3], none, none, swapped[1], none, straight[2], swapped[2], none]
    ints = jnp.concatenate([source, jnp.stack(low), jnp.stack(high), side], axis=0).astype(jnp.int32)
    on = present.astype(F32)
    shared = jnp.sum(on[4:].reshape(4, 3, slot_count), axis=1)
    nothing = jnp.zeros_like(shared[0])
    copies = jnp.stack(
        [
            shared[0], on[0], on[0], shared[1], on[3], nothing, nothing, on[1],
            on[3], nothing, nothing, on[1], shared[3], on[2], on[2], shared[2],
        ]
    )
    return source, ints, copies


def body(
    right_side,
    metric,
    mass_weight,
    helmholtz,
    vertical,
    block_inverse,
    edge_neighbour,
    edge_flip,
    corner_neighbour,
    element_count,
):
    peers = lax.axis_size("elem")
    position = lax.axis_index("elem")
    upward_elem = [(i, i + 1) for i in range(peers - 1)]
    downward_elem = [(i + 1, i) for i in range(peers - 1)]

    residual, message = call(
        begin_kernel,
        "begin",
        [scalars(), field_spec(), inverse_spec(), row_spec(16)],
        [field_spec(), tile_spec(40)],
        [struct(*FIELD), struct(8, 40, LANES)],
        [],
        1 << 22,
        (element_count, right_side, block_inverse, vertical),
    )
    coupling = lax.all_to_all(message, "lev", split_axis=0, concat_axis=0, tiled=True)
    scan_cost = pl.CostEstimate(flops=1 << 16, bytes_accessed=1 << 18, transcendentals=0)
    small = pltpu.CompilerParams(vmem_limit_bytes=SMALL_VMEM_BYTES)
    carried = pl.pallas_call(
        scan_first_kernel,
        out_shape=struct(8, 40, LANES),
        name="scan_first",
        cost_estimate=scan_cost,
        compiler_params=small,
    )(coupling)
    came = lax.all_to_all(carried, "lev", split_axis=0, concat_axis=0, tiled=True)
    below_row = came

    count_before = lax.ppermute(element_count, "elem", upward_elem)[0]
    source, ints, copies = neighbour_tables(
        edge_neighbour, edge_flip, corner_neighbour, count_before, position
    )
    own_counts, own_lists = neighbour_lists(source, 0, 8)
    far_counts, far_lists = neighbour_lists(source, 8, 3)
    forward, backward = stacked_tables()

    shared_specs = [scalars(), inverse_spec(), row_spec(16), field_spec(), tile_spec(40)]
    halo = struct(25, 8, LANES)
    smoothed, product, tail, head = call(
        lambda *refs: solve_kernel(0, False, *refs),
        "solve_first",
        shared_specs,
        [field_spec(), whole(8, LANES), whole(25, 8, LANES), whole(25, 8, LANES)],
        [struct(*FIELD), struct(8, LANES), halo, halo],
        vmem([((24, 8, LANES), F32), ((16, LANES), F32)]),
        1 << 22,
        (element_count, block_inverse, vertical, residual, came),
    )
    state = came
    solution = direction = image = flow = scalar_rows = None
    for iteration in range(ITERATIONS):
        first = iteration == 0
        last = iteration == ITERATIONS - 1
        before = lax.ppermute(tail, "elem", upward_elem)
        after = lax.ppermute(head, "elem", downward_elem)
        applied = call(
            operate_kernel,
            "operate",
            [
                scalars(), scalars(), scalars(), whole(*FIELD), row_spec(48), row_spec(16),
                pl.BlockSpec((3, NODES, LANES), lambda t: (0, 0, t)), row_spec(16), row_spec(16),
                tile_spec(40), tile_spec(state.shape[1]), whole(2, 256, 128), whole(2, 128, 256),
            ],
            field_spec(),
            struct(*FIELD),
            vmem([((24, 8, 1024), F32)] + PICK_SCRATCH),
            1 << 30,
            (
                helmholtz, own_counts, own_lists, smoothed, ints, copies, metric, mass_weight,
                vertical, below_row, state, forward, backward,
            ),
        )
        args = [
            far_counts, far_lists, applied, smoothed, ints, before, after, product, block_inverse,
            vertical,
        ]
        specs = [
            scalars(), scalars(), field_spec(), field_spec(), row_spec(48), whole(25, 8, LANES),
            whole(25, 8, LANES), whole(8, LANES), inverse_spec(), row_spec(16),
        ]
        if not first:
            args += [direction, image]
            specs += [field_spec(), field_spec()]
        applied, message = call(
            lambda *refs, first=first: image_kernel(first, *refs),
            "image_first" if first else "image",
            specs,
            [field_spec(), whole(8, 40, LANES)],
            [struct(*FIELD), struct(8, 40, LANES)],
            vmem(
                [((24, 8, 3 * LANES), F32)] + PICK_SCRATCH + [((16, LANES), F32), ((16, LANES), F32)]
            ),
            1 << 22,
            args,
        )
        received = lax.all_to_all(message, "lev", split_axis=0, concat_axis=0, tiled=True)
        carried, dots = pl.pallas_call(
            scan_kernel,
            out_shape=[struct(8, 32, LANES), struct(8, LANES)],
            name="scan",
            cost_estimate=scan_cost,
            compiler_params=small,
        )(received, coupling)
        dots = sum_over_elem(dots, peers)
        carried, dots = lax.optimization_barrier((carried, dots))
        came = lax.all_to_all(carried, "lev", split_axis=0, concat_axis=0, tiled=True)

        args = [element_count, block_inverse, vertical, residual, came, smoothed, applied, state, dots]
        specs = shared_specs[:4] + [
            tile_spec(32), field_spec(), field_spec(), tile_spec(state.shape[1]), whole(8, LANES),
        ]
        if not first:
            args += [solution, direction, image, flow, scalar_rows]
            specs += [field_spec(), field_spec(), field_spec(), tile_spec(32), whole(8, LANES)]
        out_specs = [field_spec(), field_spec(), field_spec(), whole(8, LANES)]
        shapes = [struct(*FIELD), struct(*FIELD), struct(*FIELD), struct(8, LANES)]
        if last:
            out_specs += [field_spec(), whole(LANES, LANES)]
            shapes += [struct(*FIELD), struct(LANES, LANES)]
            scratch = vmem([((16, LANES), F32)])
        else:
            out_specs += [field_spec(), tile_spec(32), tile_spec(32), field_spec(), whole(8, LANES)]
            out_specs += [whole(25, 8, LANES), whole(25, 8, LANES)]
            shapes += [struct(*FIELD), struct(8, 32, LANES), struct(8, 32, LANES), struct(*FIELD)]
            shapes += [struct(8, LANES), halo, halo]
            scratch = vmem([((24, 8, LANES), F32), ((16, LANES), F32)])
        results = call(
            lambda *refs, first=first, last=last: solve_kernel(1 if first else 2, last, *refs),
            "solve_last" if last else "solve",
            specs,
            out_specs,
            shapes,
            scratch,
            1 << 22,
            args,
        )
        if last:
            solution, residual, direction, scalar_rows, smoothed, product = results
        else:
            solution, residual, direction, scalar_rows, image, flow, state = results[:7]
            smoothed, product, tail, head = results[7:]
    norms = lax.all_to_all(product, ("elem", "lev"), split_axis=0, concat_axis=0, tiled=True)
    direction = call(
        finish_kernel,
        "finish",
        [whole(LANES, LANES), whole(8, LANES), field_spec(), field_spec()],
        field_spec(),
        struct(*FIELD),
        [],
        1 << 20,
        (norms, scalar_rows, smoothed, direction),
    )
    return (solution, residual, direction)


def solution(mesh):
    in_specs = (
        P("lev", None, "elem"),
        P(None, None, "elem"),
        P(None, "elem"),
        P("lev"),
        P("lev", "elem"),
        P("lev", None, None, "elem"),
        P("elem", None),
        P("elem", None),
        P("elem", None, None),
        P("elem"),
    )
    out_specs = (P("lev", None, "elem"), P("lev", None, "elem"), P("lev", None, "elem"))
    return jax.shard_map(body, mesh=mesh, in_specs=in_specs, out_specs=out_specs, check_vma=False)
```

```python
import math

import jax
import jax.numpy as jnp
import numpy as np
from jax import lax
from jax.experimental import pallas as pl
from jax.experimental.pallas import tpu as pltpu
from jax.sharding import PartitionSpec as P

COLUMNS = 128
ITERATIONS = 3
BORDER = COLUMNS + 1
LANES = 128
LEVELS = 16
NODES = 16
GROUPS = 8
PENALTY = 2.0
ABSENT = 15 * LANES
PLAN = 13
VMEM_BYTES = 12 * 1024 * 1024
SMALL_VMEM_BYTES = 4 * 1024 * 1024
F32 = jnp.float32
BF16 = jnp.bfloat16


def gradient_table():
    root = 1.0 / math.sqrt(5.0)
    points = [-1.0, -root, root, 1.0]
    legendre = [0.5 * (5.0 * p * p * p - 3.0 * p) for p in points]
    matrix = [[0.0 for col in range(4)] for row in range(4)]
    for row in range(4):
        for col in range(4):
            if row != col:
                matrix[row][col] = legendre[row] / (legendre[col] * (points[row] - points[col]))
    matrix[0][0] = -3.0
    matrix[3][3] = 3.0
    derivative = np.array(matrix)
    return np.kron(np.eye(4), derivative), np.kron(derivative, np.eye(4))


def stacked_tables():
    along_x, along_y = gradient_table()
    table = np.concatenate([np.kron(np.eye(8), along_x), np.kron(np.eye(8), along_y)], axis=0)
    both = np.zeros((384, 256))
    both[:256, :128] = table
    both[256:] = table.T
    both = jnp.asarray(both, F32)
    high = both.astype(BF16)
    return jnp.stack([high, (both - high.astype(F32)).astype(BF16)])


def lane_take(values, index):
    return jnp.take_along_axis(values, index, axis=1, mode="promise_in_bounds")


def row_take(values, index):
    return jnp.take_along_axis(values, index, axis=0, mode="promise_in_bounds")


def iotas():
    rows = lax.broadcasted_iota(jnp.int32, (8, LANES), 0)
    lanes = lax.broadcasted_iota(jnp.int32, (8, LANES), 1)
    return rows, lanes


def by_row(rows, values):
    index = jnp.zeros_like(rows)
    for row, value in enumerate(values):
        if value:
            index = jnp.where(rows == row, value, index)
    return index


def edge_table(low, high, rows):
    from_low = row_take(low, by_row(rows, [1, 2, 7, 0, 0, 0, 4, 0]))
    from_high = row_take(high, by_row(rows, [0, 0, 0, 3, 5, 6, 0, 0]))
    use_low = (rows < 3) | (rows == 6)
    return jnp.where(use_low, from_low, from_high)


def corner_table(low, high, low_next, high_next, rows):
    index_low = by_row(rows, [0, 3, 0, 0, 0, 3, 0, 0])
    index_high = by_row(rows, [0, 0, 7, 4, 0, 0, 7, 4])
    first = jnp.where(rows < 2, row_take(low, index_low), row_take(high, index_high))
    second = jnp.where(rows < 6, row_take(low_next, index_low), row_take(high_next, index_high))
    return jnp.where(rows < 4, first, second)


def store_tables(load, rows, put):
    for pair in range(LEVELS // 2):
        even = load(2 * pair)
        odd = load(2 * pair + 1)
        put(2 * pair, edge_table(even[:8], even[8:], rows))
        put(2 * pair + 1, edge_table(odd[:8], odd[8:], rows))
        put(LEVELS + pair, corner_table(even[:8], even[8:], odd[:8], odd[8:], rows))


def gather_pick(table, first_tile, ints, plan, far, tile, edges, corners, pick):
    rows, lanes = iotas()
    edges[...] = jnp.zeros(edges.shape, F32)
    corners[...] = jnp.zeros(corners.shape, F32)

    def step(turn, unused):
        which = plan[tile * PLAN + (10 if far else 2) + turn]
        column = pl.multiple_of((which - first_tile) * LANES, LANES)
        values = [table[member, :, pl.ds(column, LANES)] for member in range(LEVELS + 8)]
        for side in range(4):
            source = jnp.broadcast_to(ints[side : side + 1, :], (8, LANES))
            lane = jnp.bitwise_and(source, LANES - 1)
            hit = lax.shift_right_logical(source, 7) == which
            for place in range(LEVELS):
                edges[side, place] = jnp.where(
                    hit, lane_take(values[place], lane), edges[side, place]
                )
        for corner in range(4):
            sums = [corners[corner, place] for place in range(8)]
            for other in range(3):
                item = 4 + 3 * corner + other
                source = jnp.broadcast_to(ints[item : item + 1, :], (8, LANES))
                node = jnp.broadcast_to(ints[32 + item : 33 + item, :], (8, LANES))
                lane = jnp.bitwise_and(source, LANES - 1)
                hit = (lax.shift_right_logical(source, 7) == which) & (
                    jnp.bitwise_and(rows, 3) == node
                )
                for place in range(8):
                    sums[place] = sums[place] + jnp.where(
                        hit, lane_take(values[LEVELS + place], lane), 0.0
                    )
            for place in range(8):
                corners[corner, place] = sums[place]
        return unused

    lax.fori_loop(0, plan[tile * PLAN + (1 if far else 0)], step, 0)
    low_index = ints[16:24, :]
    high_index = ints[24:32, :]
    next_row = jnp.bitwise_and(rows, 4) + jnp.bitwise_and(rows + 1, 3)
    next_pair = jnp.bitwise_and(rows, 4) + jnp.bitwise_and(rows + 2, 3)
    other_half = jnp.bitwise_xor(rows, 4)
    for pair in range(LEVELS // 2):
        sums = []
        for corner in range(4):
            total = corners[corner, pair]
            total = total + row_take(total, next_row)
            total = total + row_take(total, next_pair)
            sums.append((total, row_take(total, other_half)))
        for half in range(2):
            level = 2 * pair + half
            low = jnp.where(
                (rows == 1) | (rows == 2),
                row_take(edges[0, level], low_index),
                jnp.where(
                    rows == 7,
                    row_take(edges[1, level], low_index),
                    row_take(edges[3, level], low_index),
                ),
            )
            low = jnp.where((rows == 5) | (rows == 6), 0.0, low)
            high = jnp.where(
                rows == 3,
                row_take(edges[1, level], high_index),
                jnp.where(
                    rows == 0,
                    row_take(edges[3, level], high_index),
                    row_take(edges[2, level], high_index),
                ),
            )
            high = jnp.where((rows == 1) | (rows == 2), 0.0, high)
            low = jnp.where(rows == 0, sums[0][half], jnp.where(rows == 3, sums[1][half], low))
            high = jnp.where(rows == 7, sums[2][1 - half], jnp.where(rows == 4, sums[3][1 - half], high))
            pick[level, 0:8, :] = low
            pick[level, 8:16, :] = high


def group_rows(inverse, vertical):
    link0, link1 = vertical[7:8, :], vertical[15:16, :]
    up0 = link0 * inverse[0, 7, 0:1, :]
    up1 = link1 * inverse[1, 7, 0:1, :]
    down0 = link0 * inverse[0, 0, 7:8, :]
    down1 = link1 * inverse[1, 0, 7:8, :]
    response = inverse[0, 0, 0:1, :] + down0 * inverse[1, 0, 0:1, :] * up0
    return up1 * up0, response, down0 * down1


def group_response(load, inverse, vertical):
    link0, link1 = vertical[7:8, :], vertical[15:16, :]
    down0 = link0 * inverse[0, 0, 7:8, :]
    last0 = first0 = last1 = first1 = None
    for j in range(8):
        value0, value1 = load(j), load(8 + j)
        terms = (
            inverse[0, 7, j : j + 1, :] * value0,
            inverse[0, 0, j : j + 1, :] * value0,
            inverse[1, 7, j : j + 1, :] * value1,
            inverse[1, 0, j : j + 1, :] * value1,
        )
        if j == 0:
            last0, first0, last1, first1 = terms
        else:
            last0, first0, last1, first1 = (
                last0 + terms[0],
                first0 + terms[1],
                last1 + terms[2],
                first1 + terms[3],
            )
    carried = link0 * last0
    upward = link1 * (last1 + inverse[1, 7, 0:1, :] * carried)
    downward = first0 + down0 * (first1 + inverse[1, 0, 0:1, :] * carried)
    return upward, downward


def total_of(values):
    return jnp.sum(jnp.sum(values, axis=1, keepdims=True), axis=0, keepdims=True)


def begin_kernel(count, right_side, inverse, vertical, residual, message):
    tile = pl.program_id(0)
    lanes = lax.broadcasted_iota(jnp.int32, (NODES, LANES), 1)
    living = lanes + tile * LANES < count[0]

    for level in range(LEVELS):
        residual[level] = jnp.where(living, right_side[level], 0.0)
    upward, downward = group_response(lambda level: residual[level], inverse, vertical)
    message[0, 0:16, :] = upward
    message[0, 16:32, :] = downward
    coupling = group_rows(inverse, vertical)
    for row in range(3):
        message[0, 32 + row : 33 + row, :] = coupling[row]
    link = vertical[15:16, :]
    message[0, 35:36, :] = link * (link * inverse[1, 7, 7:8, :] - 1.0)
    message[0, 36:40, :] = jnp.zeros((4, LANES), F32)


def joined(first, last, *refs):
    refs = list(refs)
    flags, seg, got, inner = refs[:4]
    del refs[:4]
    if first:
        aux = refs.pop(0)
    else:
        terms = refs.pop(0)
    if last:
        own = refs.pop(0)
        if not first:
            ends = refs.pop(0)
        carried = refs.pop(0)
    else:
        seg_out, inner_out = refs.pop(0), refs.pop(0)
    if first:
        terms, aux_out = refs.pop(0), refs.pop(0)
        if last:
            ends = refs.pop(0)

    def row(ref, tile, index):
        return ref[tile, index : index + 1, :]

    def finish(tile, below, above_up, above_down):
        if last:
            leaving = row(ends, tile, 1) * below + own[tile, 0:16, :]
            carried[tile, 0:16, :] = below
            carried[tile, 16:32, :] = above_down + row(ends, tile, 0) * leaving
        else:
            inner_out[tile, 0:16, :] = below
            inner_out[tile, 16:32, :] = above_up
            inner_out[tile, 32:48, :] = above_down

    def prepare(tile, partner_below):
        for index in range(3):
            terms[tile, index : index + 1, :] = row(got, tile, 32 + index)
            terms[tile, 3 + index : 4 + index, :] = row(seg, tile, 32 + index)
        terms[tile, 6:7, :] = row(aux, tile, 0)
        terms[tile, 7:8, :] = row(aux, tile, 3)
        up_p, both_p, down_p, up, both, down = [row(terms, tile, index) for index in range(6)]
        below, above, through, back, flow = [row(aux, tile, index) for index in range(5)]
        if partner_below:
            bottom = jnp.broadcast_to(flags[1], flow.shape)
            flow = jnp.where(bottom == 1, row(got, tile, 35), flow)
            below = below * up_p
            joint = (up * up_p, both_p + down_p * both * up_p, down_p * down, row(seg, tile, 35))
        else:
            through = through + back * both_p * above
            above = up_p * above
            back = back * down_p
            joint = (up_p * up, both + down * both_p * up, down * down_p, row(got, tile, 35))
        for index, value in enumerate((below, above, through, back, flow)):
            aux_out[tile, index : index + 1, :] = value
        aux_out[tile, 5:8, :] = jnp.zeros((3, LANES), F32)
        if last:
            ends[tile, 0:1, :] = through
            ends[tile, 1:2, :] = row(own, tile, 32)
            ends[tile, 2:8, :] = jnp.zeros((6, LANES), F32)
        else:
            for index, value in enumerate(joint):
                seg_out[tile, 32 + index : 33 + index, :] = value
            seg_out[tile, 36:40, :] = jnp.zeros((4, LANES), F32)

    @pl.when(flags[0] == 1)
    def partner_below():
        for tile in range(GROUPS):
            if first:
                prepare(tile, True)
            came_up, came_down = got[tile, 0:16, :], got[tile, 16:32, :]
            if not last:
                upward, downward = seg[tile, 0:16, :], seg[tile, 16:32, :]
                seg_out[tile, 0:16, :] = row(terms, tile, 3) * came_up + upward
                seg_out[tile, 16:32, :] = came_down + row(terms, tile, 2) * (
                    downward + row(terms, tile, 4) * came_up
                )
            below = row(terms, tile, 6) * came_up + inner[tile, 0:16, :]
            finish(tile, below, inner[tile, 16:32, :], inner[tile, 32:48, :])

    @pl.when(flags[0] != 1)
    def partner_above():
        for tile in range(GROUPS):
            if first:
                prepare(tile, False)
            came_up, came_down = got[tile, 0:16, :], got[tile, 16:32, :]
            if not last:
                upward, downward = seg[tile, 0:16, :], seg[tile, 16:32, :]
                seg_out[tile, 0:16, :] = row(terms, tile, 0) * upward + came_up
                seg_out[tile, 16:32, :] = downward + row(terms, tile, 5) * (
                    came_down + row(terms, tile, 1) * upward
                )
            above_up, above_down = inner[tile, 16:32, :], inner[tile, 32:48, :]
            finish(
                tile,
                inner[tile, 0:16, :],
                row(terms, tile, 0) * above_up + came_up,
                above_down + row(terms, tile, 7) * (came_down + row(terms, tile, 1) * above_up),
            )


def solve_kernel(stage, last, *refs):
    refs = list(refs)

    def take(count):
        taken = refs[:count]
        del refs[:count]
        return taken

    count, inverse, vertical, residual_in, came = take(5)
    if stage:
        smoothed_in, applied, state_in = take(3)
        dot_parts = take(2)
    if stage == 2:
        solution_in, direction_in, image_in, flow_in, scalars_in = take(5)
    if stage:
        solution, residual, direction, scalars_out = take(4)
        if not last:
            image, flow, state = take(3)
    else:
        residual, state = residual_in, came
    smoothed, product = take(2)
    if not last:
        near, far, tables = take(3)
    (parts,) = take(1)
    tile = pl.program_id(0)
    rows, lanes = iotas()

    if stage:
        dots = dot_parts[0][...] + dot_parts[1][...]
        norm = jnp.sum(dots[0:1, :], axis=1, keepdims=True)
        curvature = jnp.sum(dots[1:2, :], axis=1, keepdims=True)
        if stage == 2:
            cross = jnp.sum(dots[2:3, :], axis=1, keepdims=True)
            ratio = norm / scalars_in[0:1, 0:1]
            curvature = curvature + ratio * cross + ratio * ratio * scalars_in[1:2, 0:1]
        step_size = norm / curvature
        scalars_out[0:1, :] = jnp.broadcast_to(norm, (1, LANES))
        scalars_out[1:2, :] = jnp.broadcast_to(curvature, (1, LANES))
        scalars_out[2:8, :] = jnp.zeros((6, LANES), F32)
        for level in range(LEVELS):
            value = smoothed_in[level]
            result = applied[level]
            if stage == 2:
                value = value + ratio * direction_in[level]
                result = result + ratio * image_in[level]
                solution[level] = solution_in[level] + step_size * value
            else:
                solution[level] = step_size * value
            direction[level] = value
            if not last:
                image[level] = result
            residual[level] = residual_in[level] - step_size * result
        change = came[0, 0:32, :]
        if stage == 2:
            change = change + ratio * flow_in[0]
        incoming = state_in[0, 0:32, :] - step_size * change
        if not last:
            flow[0] = change
            state[0] = incoming
    else:
        incoming = came[0, 0:32, :]
    link0, link1 = vertical[7:8, :], vertical[15:16, :]
    below = incoming[0:16]
    above = incoming[16:32]

    def block_product(block, lifted):
        solved = []
        for i in range(8):
            total = inverse[block, i, 0:1, :] * lifted[0]
            for j in range(1, 8):
                total = total + inverse[block, i, j : j + 1, :] * lifted[j]
            solved.append(total)
        return solved

    values = [residual[level] for level in range(8)]
    lower = block_product(0, [values[0] + below] + values[1:])
    values = [residual[8 + level] for level in range(8)]
    upper = block_product(1, [values[0] + link0 * lower[7]] + values[1:])
    lift = link1 * above
    upper = [upper[i] + lift * inverse[1, i, 7:8, :] for i in range(8)]
    lift = link0 * upper[0]
    lower = [lower[i] + lift * inverse[0, i, 7:8, :] for i in range(8)]
    total = None
    for level, value in enumerate(lower + upper):
        smoothed[level] = value
        term = value * residual[level]
        total = term if total is None else total + term

    @pl.when(tile == 0)
    def clear():
        parts[...] = jnp.zeros((16, LANES), F32)

    parts[...] += total

    @pl.when(tile == GROUPS - 1)
    def finish():
        product[...] = jnp.broadcast_to(jnp.sum(parts[...], axis=0, keepdims=True), product.shape)

    if last:
        return

    start = count[0] - LANES
    start_tile = lax.shift_right_logical(start, 7)
    offset = jnp.bitwise_and(start, LANES - 1)
    extra = start - 1
    extra_tile = lax.shift_right_logical(extra, 7)
    extra_lane = jnp.bitwise_and(extra, LANES - 1)
    in_tail = (tile == start_tile) | (tile == start_tile + 1)
    in_extra = tile == extra_tile

    def put(position, value):
        tables[position] = value

    @pl.when(in_tail | in_extra | (tile < 2))
    def build():
        store_tables(lambda level: smoothed[level], rows, put)

    def fill(tail, head):
        @pl.when(tile == 0)
        def clear_tail():
            tail[...] = jnp.zeros((25, 8, LANES), F32)
            head[...] = jnp.zeros((25, 8, LANES), F32)

        @pl.when(in_tail)
        def fill_tail():
            index = jnp.bitwise_and(lanes + offset, LANES - 1)
            before_wrap = (lanes < LANES - offset).astype(jnp.int32)
            wanted = before_wrap == (tile == start_tile).astype(jnp.int32)
            for position in range(24):
                tail[position] = jnp.where(
                    wanted, lane_take(tables[position], index), tail[position]
                )

        @pl.when(in_extra)
        def fill_extra():
            index = jnp.zeros_like(lanes) + extra_lane
            packed = jnp.zeros((8, LANES), F32)
            for position in range(24):
                packed = jnp.where(lanes == position, lane_take(tables[position], index), packed)
            tail[24] = packed

        @pl.when(tile == 0)
        def fill_head():
            for position in range(24):
                head[position] = tables[position]

        @pl.when(tile == 1)
        def fill_head_extra():
            packed = jnp.zeros((8, LANES), F32)
            for position in range(24):
                packed = jnp.where(
                    lanes == position, lane_take(tables[position], jnp.zeros_like(lanes)), packed
                )
            head[24] = packed

    odd = jnp.bitwise_and(count[1], 1)
    pl.when(odd == 0)(lambda: fill(near, far))
    pl.when(odd == 1)(lambda: fill(far, near))


def finish_kernel(norms, scalars_in, smoothed, direction_in, direction):
    ratio = total_of(norms[...]) / scalars_in[0:1, 0:1]
    for level in range(LEVELS):
        direction[level] = smoothed[level] + ratio * direction_in[level]


def split(values):
    high = values.astype(BF16)
    return high, (values - high.astype(F32)).astype(BF16)


def product3(tables, rows, columns, values):
    high, low = split(values)
    result = jnp.dot(tables[0, rows, columns], high, preferred_element_type=F32)
    result = result + jnp.dot(tables[0, rows, columns], low, preferred_element_type=F32)
    return result + jnp.dot(tables[1, rows, columns], high, preferred_element_type=F32)


def operate_kernel(
    helmholtz,
    plan,
    field,
    ints,
    copies,
    metric,
    mass,
    vertical,
    below_row,
    state,
    tables,
    applied,
    table,
    edges,
    corners,
    pick,
):
    tile = pl.program_id(0)
    rows, lanes = iotas()
    here = pl.ds(pl.multiple_of(tile * LANES, LANES), LANES)

    @pl.when(tile == 0)
    def build():
        def one(part, unused):
            there = pl.ds(pl.multiple_of(part * LANES, LANES), LANES)

            def put(position, value):
                table[position, :, there] = value

            store_tables(lambda level: field[level, :, there], rows, put)
            return unused

        lax.fori_loop(0, GROUPS, one, 0)

    gather_pick(table, 0, ints, plan, False, tile, edges, corners, pick)
    mixed, along_y, along_x = metric[1], metric[2], metric[0]
    for half in range(2):
        values = jnp.concatenate([field[8 * half + level, :, here] for level in range(8)], axis=0)
        gradients = product3(tables, slice(0, 256), slice(0, 128), values)
        flux_x = []
        flux_y = []
        for level in range(8):
            part_x = gradients[16 * level : 16 * level + 16]
            part_y = gradients[128 + 16 * level : 144 + 16 * level]
            flux_x.append(along_x * part_x + mixed * part_y)
            flux_y.append(mixed * part_x + along_y * part_y)
        stiff = product3(tables, slice(256, 384), slice(0, 256), jnp.concatenate(flux_x + flux_y, axis=0))
        for level in range(8):
            applied[8 * half + level] = stiff[16 * level : 16 * level + 16]
    twice = PENALTY * copies[...]
    flux = state[0, 0:16, :] + below_row[0, 4:5, :] * field[0, :, here]
    for level in range(LEVELS):
        value = field[level, :, here]
        higher = field[level + 1, :, here] if level < LEVELS - 1 else state[0, 16:32, :]
        next_flux = vertical[level : level + 1, :] * (value - higher)
        applied[level] = (
            applied[level]
            + (helmholtz[level] * mass[...] + twice) * value
            + (next_flux - flux)
            - PENALTY * pick[level]
        )
        flux = next_flux


def image_kernel(first, *refs):
    count, plan, applied, smoothed, ints, near, far, product, inverse, vertical = refs[:10]
    refs = refs[10:]
    if not first:
        direction, previous = refs[:2]
        refs = refs[2:]
    image, message, dots, table, edges, corners, pick, parts, crosses = refs
    tile = pl.program_id(0)
    rows, lanes = iotas()

    @pl.when(tile == 0)
    def build():
        parts[...] = jnp.zeros((16, LANES), F32)
        crosses[...] = jnp.zeros((16, LANES), F32)

        def fill(before, after):
            for position in range(24):
                index = jnp.full((8, LANES), position, jnp.int32)
                table[position, :, 0:LANES] = before[position]
                table[position, :, LANES : 2 * LANES] = after[position]
                table[position, :, 2 * LANES : 3 * LANES] = jnp.where(
                    lanes == 0, lane_take(before[24], index), lane_take(after[24], index)
                )

        odd = jnp.bitwise_and(count[1], 1)
        pl.when(odd == 0)(lambda: fill(far, near))
        pl.when(odd == 1)(lambda: fill(near, far))

    pick[...] = jnp.zeros((LEVELS, NODES, LANES), F32)

    @pl.when(plan[tile * PLAN + 1] > 0)
    def reach():
        gather_pick(table, 8, ints, plan, True, tile, edges, corners, pick)

    total = cross = None
    for level in range(LEVELS):
        value = smoothed[level]
        result = applied[level] - PENALTY * pick[level]
        image[level] = result
        term = value * result
        total = term if total is None else total + term
        if not first:
            term = value * previous[level] + direction[level] * result
            cross = term if cross is None else cross + term
    parts[...] += total
    if not first:
        crosses[...] += cross
    upward, downward = group_response(lambda level: image[level], inverse, vertical)
    message[0, 0:16, :] = upward
    message[0, 16:32, :] = downward

    @pl.when(tile == GROUPS - 1)
    def finish():
        dots[0:1, :] = product[0:1, :]
        dots[1:2, :] = jnp.sum(parts[...], axis=0, keepdims=True)
        dots[2:3, :] = jnp.sum(crosses[...], axis=0, keepdims=True)
        dots[3:8, :] = jnp.zeros((5, LANES), F32)


def field_spec():
    return pl.BlockSpec((LEVELS, NODES, LANES), lambda t: (0, 0, t))


def row_spec(rows):
    return pl.BlockSpec((rows, LANES), lambda t: (0, t))


def whole(*shape):
    return pl.BlockSpec(shape, lambda t: (0,) * len(shape))


def tile_spec(rows):
    return pl.BlockSpec((1, rows, LANES), lambda t: (t, 0, 0))


def inverse_spec():
    return pl.BlockSpec((2, 8, 8, LANES), lambda t: (0, 0, 0, t))


def scalars():
    return pl.BlockSpec(memory_space=pltpu.SMEM)


def struct(*shape):
    return jax.ShapeDtypeStruct(shape, F32)


def call(kernel, name, in_specs, out_specs, out_shape, scratch, cost, args):
    return pl.pallas_call(
        kernel,
        grid=(GROUPS,),
        in_specs=in_specs,
        out_specs=out_specs,
        out_shape=out_shape,
        scratch_shapes=scratch,
        name=name,
        compiler_params=pltpu.CompilerParams(
            dimension_semantics=("arbitrary",), vmem_limit_bytes=VMEM_BYTES
        ),
        cost_estimate=pl.CostEstimate(flops=cost, bytes_accessed=6 << 20, transcendentals=0),
    )(*args)


FIELD = (LEVELS, NODES, 1024)
PICK_SCRATCH = [
    ((4, LEVELS, 8, LANES), F32),
    ((4, 8, 8, LANES), F32),
    ((LEVELS, NODES, LANES), F32),
]


def vmem(shapes):
    return [pltpu.VMEM(shape, dtype) for shape, dtype in shapes]


def prepare_kernel(place, edge_rows, flip_rows, corner_rows, ints, copies):
    position, count_before = place[0], place[1]

    def source_of(entry):
        element = lax.shift_right_logical(entry, 2)
        holder = lax.shift_right_logical(element, 10)
        within = jnp.bitwise_and(element, 1023)
        earlier = within - (count_before - BORDER)
        earlier = jnp.where(earlier == 0, 10 * LANES, 8 * LANES + earlier - 1)
        later = jnp.where(within < LANES, 9 * LANES + within, 10 * LANES + 1)
        source = jnp.where(holder == position, within, jnp.where(holder < position, earlier, later))
        return jnp.where(entry >= 0, source, ABSENT)

    edges, corners = edge_rows[...], corner_rows[...]
    ints[0:4, :] = source_of(edges)
    ints[4:16, :] = source_of(corners)
    flipped = (flip_rows[...] == 1).astype(jnp.int32)
    straight = 2 * jnp.bitwise_and(edges, 3) + flipped
    swapped_row = 2 * jnp.bitwise_and(edges, 3) + 1 - flipped
    none = jnp.zeros((1, LANES), jnp.int32)

    def of(rows, side):
        return rows[side : side + 1, :]

    low = [none, of(straight, 0), of(swapped_row, 0), none, of(straight, 3), none, none, of(straight, 1)]
    high = [of(swapped_row, 3), none, none, of(swapped_row, 1), none, of(straight, 2),
            of(swapped_row, 2), none]
    for row, value in enumerate(low + high):
        ints[16 + row : 17 + row, :] = value
    ints[32:36, :] = jnp.zeros((4, LANES), jnp.int32)
    ints[36:48, :] = jnp.bitwise_and(corners, 3)
    on = (edges >= 0).astype(F32)
    there = (corners >= 0).astype(F32)
    shared = [
        of(there, 3 * corner) + of(there, 3 * corner + 1) + of(there, 3 * corner + 2)
        for corner in range(4)
    ]
    zero = jnp.zeros((1, LANES), F32)
    rows = [
        shared[0], of(on, 0), of(on, 0), shared[1], of(on, 3), zero, zero, of(on, 1),
        of(on, 3), zero, zero, of(on, 1), shared[3], of(on, 2), of(on, 2), shared[2],
    ]
    for row, value in enumerate(rows):
        copies[row : row + 1, :] = value


def gather_plan(ints):
    holder = (ints[:16] // LANES).reshape(16, 8, LANES)
    tiles = jnp.arange(11, dtype=jnp.int32)
    used = jnp.any(holder[:, :, None, :] == tiles[None, None, :, None], axis=(0, 3))
    far = tiles >= 8
    same = far[:, None] == far[None, :]
    earlier = used[:, None, :] & (same & (tiles[None, :] < tiles[:, None]))[None]
    place = jnp.sum(earlier.astype(jnp.int32), axis=2) + jnp.where(far, 10, 2)[None]
    columns = jnp.arange(PLAN, dtype=jnp.int32)
    listed = (place[:, :, None] == columns) * tiles[None, :, None]
    counted = columns[None, :] == jnp.where(far, 1, 0)[:, None]
    values = jnp.where(used[:, :, None], listed + counted[None].astype(jnp.int32), 0)
    return jnp.sum(values, axis=1).astype(jnp.int32).reshape(-1)


def parts_along(value, peers, inner):
    side = math.isqrt(peers)
    parts = []
    for shift in range(1, side):
        pairs = []
        for i in range(peers):
            outer, within = i // side, i % side
            if inner:
                pairs.append((i, outer * side + (within ^ shift)))
            else:
                pairs.append((i, (outer ^ shift) * side + within))
        parts.append(lax.ppermute(value, "elem", pairs))
    return parts


def swapped(value, distance):
    return lax.ppermute(value, "lev", [(i, i ^ distance) for i in range(GROUPS)])


def join(name, first, last, shapes, args):
    return pl.pallas_call(
        lambda *refs: joined(first, last, *refs),
        in_specs=[scalars()] + [pl.BlockSpec(memory_space=pltpu.VMEM)] * (len(args) - 1),
        out_shape=[struct(8, rows, LANES) for rows in shapes],
        name=name,
        cost_estimate=pl.CostEstimate(flops=1 << 16, bytes_accessed=1 << 18, transcendentals=0),
        compiler_params=pltpu.CompilerParams(vmem_limit_bytes=SMALL_VMEM_BYTES),
    )(*args)


def body(
    right_side,
    metric,
    mass_weight,
    helmholtz,
    vertical,
    block_inverse,
    edge_neighbour,
    edge_flip,
    corner_neighbour,
    element_count,
):
    peers = lax.axis_size("elem")
    position = lax.axis_index("elem")
    upward_elem = [(i, i + 1) for i in range(peers - 1)]
    near_pairs = [(i, i ^ 1) for i in range(peers)]
    far_pairs = [(i, i - 1 if i % 2 == 0 else i + 1) for i in range(1, peers - 1)]
    count = jnp.concatenate([element_count, position.astype(jnp.int32)[None]])

    residual, message = call(
        begin_kernel,
        "begin",
        [scalars(), field_spec(), inverse_spec(), row_spec(16)],
        [field_spec(), tile_spec(40)],
        [struct(*FIELD), struct(8, 40, LANES)],
        [],
        1 << 22,
        (element_count, right_side, block_inverse, vertical),
    )
    group = lax.axis_index("lev")
    flags = [
        jnp.stack([(group >> step) & 1, ((group & (2**step - 1)) == 0).astype(jnp.int32)])
        for step in range(3)
    ]
    ones = jnp.ones((8, 1, LANES), F32)
    nothing = jnp.zeros((8, 1, LANES), F32)
    aux = jnp.concatenate([ones, ones, nothing, ones] + [nothing] * 4, axis=1)
    empty = jnp.zeros((8, 48, LANES), F32)
    terms = [None] * 3
    seg, inner = message, empty
    for step in range(2):
        got = swapped(seg, 2**step)
        seg, inner, terms[step], aux = join(
            "join_first", True, False, [40, 48, 8, 8], (flags[step], seg, got, inner, aux)
        )
    got = swapped(seg, 4)
    came, terms[2], below_row, ends = join(
        "join_first_last", True, True, [32, 8, 8, 8], (flags[2], seg, got, inner, aux, message)
    )

    count_before = lax.ppermute(element_count, "elem", upward_elem)[0]
    ints, copies = call(
        prepare_kernel,
        "prepare",
        [scalars(), row_spec(4), row_spec(4), row_spec(12)],
        [row_spec(48), row_spec(16)],
        [jax.ShapeDtypeStruct((48, 1024), jnp.int32), struct(16, 1024)],
        [],
        1 << 18,
        (
            jnp.stack([position, count_before]).astype(jnp.int32),
            jnp.transpose(edge_neighbour),
            jnp.transpose(edge_flip),
            jnp.transpose(corner_neighbour, (1, 2, 0)).reshape(12, 1024),
        ),
    )
    plan = gather_plan(ints)
    tables = stacked_tables()

    shared_specs = [scalars(), inverse_spec(), row_spec(16), field_spec(), tile_spec(32)]
    halo = struct(25, 8, LANES)
    smoothed, product, near, far = call(
        lambda *refs: solve_kernel(0, False, *refs),
        "solve_first",
        shared_specs,
        [field_spec(), whole(8, LANES), whole(25, 8, LANES), whole(25, 8, LANES)],
        [struct(*FIELD), struct(8, LANES), halo, halo],
        vmem([((24, 8, LANES), F32), ((16, LANES), F32)]),
        1 << 22,
        (count, block_inverse, vertical, residual, came),
    )
    state = came
    solution = direction = image = flow = scalar_rows = None
    for iteration in range(ITERATIONS):
        first = iteration == 0
        last = iteration == ITERATIONS - 1
        near = lax.ppermute(near, "elem", near_pairs)
        far = lax.ppermute(far, "elem", far_pairs)
        applied = call(
            operate_kernel,
            "operate",
            [
                scalars(), scalars(), whole(*FIELD), row_spec(48), row_spec(16),
                pl.BlockSpec((3, NODES, LANES), lambda t: (0, 0, t)), row_spec(16), row_spec(16),
                tile_spec(8), tile_spec(32), whole(2, 384, 256),
            ],
            field_spec(),
            struct(*FIELD),
            vmem([((24, 8, 1024), F32)] + PICK_SCRATCH),
            1 << 30,
            (
                helmholtz, plan, smoothed, ints, copies, metric, mass_weight,
                vertical, below_row, state, tables,
            ),
        )
        args = [
            count, plan, applied, smoothed, ints, near, far, product, block_inverse,
            vertical,
        ]
        specs = [
            scalars(), scalars(), field_spec(), field_spec(), row_spec(48), whole(25, 8, LANES),
            whole(25, 8, LANES), whole(8, LANES), inverse_spec(), row_spec(16),
        ]
        if not first:
            args += [direction, image]
            specs += [field_spec(), field_spec()]
        applied, message, dots = call(
            lambda *refs, first=first: image_kernel(first, *refs),
            "image_first" if first else "image",
            specs,
            [field_spec(), tile_spec(32), whole(8, LANES)],
            [struct(*FIELD), struct(8, 32, LANES), struct(8, LANES)],
            vmem(
                [((24, 8, 3 * LANES), F32)] + PICK_SCRATCH + [((16, LANES), F32), ((16, LANES), F32)]
            ),
            1 << 22,
            args,
        )
        seg, inner = message, empty
        for step in range(2):
            got = swapped(seg, 2**step)
            others = parts_along(dots, peers, step == 0)
            got, *others = lax.optimization_barrier((got, *others))
            dots = (dots + others[0]) + (others[1] + others[2])
            seg, inner = join(
                "join", False, False, [32, 48], (flags[step], seg, got, inner, terms[step])
            )
        got = swapped(seg, 4)
        other = swapped(dots, 4)
        got, other = lax.optimization_barrier((got, other))
        dots = dots + other
        (came,) = join(
            "join_last", False, True, [32], (flags[2], seg, got, inner, terms[2], message, ends)
        )
        dots = dots + swapped(dots, 2)
        dots = [dots, swapped(dots, 1)]

        args = [count, block_inverse, vertical, residual, came, smoothed, applied, state] + dots
        specs = shared_specs + [field_spec(), field_spec(), tile_spec(32)] + [whole(8, LANES)] * 2
        if not first:
            args += [solution, direction, image, flow, scalar_rows]
            specs += [field_spec(), field_spec(), field_spec(), tile_spec(32), whole(8, LANES)]
        out_specs = [field_spec(), field_spec(), field_spec(), whole(8, LANES)]
        shapes = [struct(*FIELD), struct(*FIELD), struct(*FIELD), struct(8, LANES)]
        if last:
            out_specs += [field_spec(), whole(LANES, LANES)]
            shapes += [struct(*FIELD), struct(LANES, LANES)]
            scratch = vmem([((16, LANES), F32)])
        else:
            out_specs += [field_spec(), tile_spec(32), tile_spec(32), field_spec(), whole(8, LANES)]
            out_specs += [whole(25, 8, LANES), whole(25, 8, LANES)]
            shapes += [struct(*FIELD), struct(8, 32, LANES), struct(8, 32, LANES), struct(*FIELD)]
            shapes += [struct(8, LANES), halo, halo]
            scratch = vmem([((24, 8, LANES), F32), ((16, LANES), F32)])
        results = call(
            lambda *refs, first=first, last=last: solve_kernel(1 if first else 2, last, *refs),
            "solve_last" if last else "solve",
            specs,
            out_specs,
            shapes,
            scratch,
            1 << 22,
            args,
        )
        if last:
            solution, residual, direction, scalar_rows, smoothed, product = results
        else:
            solution, residual, direction, scalar_rows, image, flow, state = results[:7]
            smoothed, product, near, far = results[7:]
    norms = lax.all_to_all(product, ("elem", "lev"), split_axis=0, concat_axis=0, tiled=True)
    direction = call(
        finish_kernel,
        "finish",
        [whole(LANES, LANES), whole(8, LANES), field_spec(), field_spec()],
        field_spec(),
        struct(*FIELD),
        [],
        1 << 20,
        (norms, scalar_rows, smoothed, direction),
    )
    return (solution, residual, direction)


def solution(mesh):
    in_specs = (
        P("lev", None, "elem"),
        P(None, None, "elem"),
        P(None, "elem"),
        P("lev"),
        P("lev", "elem"),
        P("lev", None, None, "elem"),
        P("elem", None),
        P("elem", None),
        P("elem", None, None),
        P("elem"),
    )
    out_specs = (P("lev", None, "elem"), P("lev", None, "elem"), P("lev", None, "elem"))
    return jax.shard_map(body, mesh=mesh, in_specs=in_specs, out_specs=out_specs, check_vma=False)
```

```python
import math

import jax
import jax.numpy as jnp
import numpy as np
from jax import lax
from jax.experimental import pallas as pl
from jax.experimental.pallas import tpu as pltpu
from jax.sharding import PartitionSpec as P

COLUMNS = 128
ITERATIONS = 3
BORDER = COLUMNS + 1
LANES = 128
LEVELS = 16
NODES = 16
GROUPS = 8
PENALTY = 2.0
ABSENT = 15 * LANES
PLAN = 13
VMEM_BYTES = 12 * 1024 * 1024
SMALL_VMEM_BYTES = 4 * 1024 * 1024
F32 = jnp.float32
BF16 = jnp.bfloat16


def gradient_table():
    root = 1.0 / math.sqrt(5.0)
    points = [-1.0, -root, root, 1.0]
    legendre = [0.5 * (5.0 * p * p * p - 3.0 * p) for p in points]
    matrix = [[0.0 for col in range(4)] for row in range(4)]
    for row in range(4):
        for col in range(4):
            if row != col:
                matrix[row][col] = legendre[row] / (legendre[col] * (points[row] - points[col]))
    matrix[0][0] = -3.0
    matrix[3][3] = 3.0
    derivative = np.array(matrix)
    return np.kron(np.eye(4), derivative), np.kron(derivative, np.eye(4))


def stacked_tables():
    along_x, along_y = gradient_table()
    table = np.concatenate([np.kron(np.eye(8), along_x), np.kron(np.eye(8), along_y)], axis=0)
    both = np.zeros((384, 256))
    both[:256, :128] = table
    both[256:] = table.T
    both = jnp.asarray(both, F32)
    high = both.astype(BF16)
    return jnp.stack([high, (both - high.astype(F32)).astype(BF16)])


def lane_take(values, index):
    return jnp.take_along_axis(values, index, axis=1, mode="promise_in_bounds")


def row_take(values, index):
    return jnp.take_along_axis(values, index, axis=0, mode="promise_in_bounds")


def iotas():
    rows = lax.broadcasted_iota(jnp.int32, (8, LANES), 0)
    lanes = lax.broadcasted_iota(jnp.int32, (8, LANES), 1)
    return rows, lanes


def by_row(rows, values):
    index = jnp.zeros_like(rows)
    for row, value in enumerate(values):
        if value:
            index = jnp.where(rows == row, value, index)
    return index


def edge_table(low, high, rows):
    from_low = row_take(low, by_row(rows, [1, 2, 7, 0, 0, 0, 4, 0]))
    from_high = row_take(high, by_row(rows, [0, 0, 0, 3, 5, 6, 0, 0]))
    use_low = (rows < 3) | (rows == 6)
    return jnp.where(use_low, from_low, from_high)


def corner_table(low, high, low_next, high_next, rows):
    index_low = by_row(rows, [0, 3, 0, 0, 0, 3, 0, 0])
    index_high = by_row(rows, [0, 0, 7, 4, 0, 0, 7, 4])
    first = jnp.where(rows < 2, row_take(low, index_low), row_take(high, index_high))
    second = jnp.where(rows < 6, row_take(low_next, index_low), row_take(high_next, index_high))
    return jnp.where(rows < 4, first, second)


def store_tables(load, rows, put):
    for pair in range(LEVELS // 2):
        even = load(2 * pair)
        odd = load(2 * pair + 1)
        put(2 * pair, edge_table(even[:8], even[8:], rows))
        put(2 * pair + 1, edge_table(odd[:8], odd[8:], rows))
        put(LEVELS + pair, corner_table(even[:8], even[8:], odd[:8], odd[8:], rows))


def gather_pick(table, first_tile, ints, plan, far, tile, edges, corners, pick):
    rows, lanes = iotas()
    edges[...] = jnp.zeros(edges.shape, F32)
    corners[...] = jnp.zeros(corners.shape, F32)

    def step(turn, unused):
        entry = plan[tile * PLAN + (10 if far else 2) + turn]
        which = jnp.bitwise_and(entry, 15)
        column = pl.multiple_of((which - first_tile) * LANES, LANES)
        values = [table[member, :, pl.ds(column, LANES)] for member in range(LEVELS + 8)]
        @pl.when(entry >= 16)
        def sides():
            for side in range(4):
                source = jnp.broadcast_to(ints[side : side + 1, :], (8, LANES))
                lane = jnp.bitwise_and(source, LANES - 1)
                hit = lax.shift_right_logical(source, 7) == which
                for place in range(LEVELS):
                    edges[side, place] = jnp.where(
                        hit, lane_take(values[place], lane), edges[side, place]
                    )

        for corner in range(4):
            sums = [corners[corner, place] for place in range(8)]
            for other in range(3):
                item = 4 + 3 * corner + other
                source = jnp.broadcast_to(ints[item : item + 1, :], (8, LANES))
                node = jnp.broadcast_to(ints[32 + item : 33 + item, :], (8, LANES))
                lane = jnp.bitwise_and(source, LANES - 1)
                hit = (lax.shift_right_logical(source, 7) == which) & (
                    jnp.bitwise_and(rows, 3) == node
                )
                for place in range(8):
                    sums[place] = sums[place] + jnp.where(
                        hit, lane_take(values[LEVELS + place], lane), 0.0
                    )
            for place in range(8):
                corners[corner, place] = sums[place]
        return unused

    lax.fori_loop(0, plan[tile * PLAN + (1 if far else 0)], step, 0)
    low_index = ints[16:24, :]
    high_index = ints[24:32, :]
    next_row = jnp.bitwise_and(rows, 4) + jnp.bitwise_and(rows + 1, 3)
    next_pair = jnp.bitwise_and(rows, 4) + jnp.bitwise_and(rows + 2, 3)
    other_half = jnp.bitwise_xor(rows, 4)
    for pair in range(LEVELS // 2):
        sums = []
        for corner in range(4):
            total = corners[corner, pair]
            total = total + row_take(total, next_row)
            total = total + row_take(total, next_pair)
            sums.append((total, row_take(total, other_half)))
        for half in range(2):
            level = 2 * pair + half
            low = jnp.where(
                (rows == 1) | (rows == 2),
                row_take(edges[0, level], low_index),
                jnp.where(
                    rows == 7,
                    row_take(edges[1, level], low_index),
                    row_take(edges[3, level], low_index),
                ),
            )
            low = jnp.where((rows == 5) | (rows == 6), 0.0, low)
            high = jnp.where(
                rows == 3,
                row_take(edges[1, level], high_index),
                jnp.where(
                    rows == 0,
                    row_take(edges[3, level], high_index),
                    row_take(edges[2, level], high_index),
                ),
            )
            high = jnp.where((rows == 1) | (rows == 2), 0.0, high)
            low = jnp.where(rows == 0, sums[0][half], jnp.where(rows == 3, sums[1][half], low))
            high = jnp.where(rows == 7, sums[2][1 - half], jnp.where(rows == 4, sums[3][1 - half], high))
            pick[level, 0:8, :] = low
            pick[level, 8:16, :] = high


def group_rows(inverse, vertical):
    link0, link1 = vertical[7:8, :], vertical[15:16, :]
    up0 = link0 * inverse[0, 7, 0:1, :]
    up1 = link1 * inverse[1, 7, 0:1, :]
    down0 = link0 * inverse[0, 0, 7:8, :]
    down1 = link1 * inverse[1, 0, 7:8, :]
    response = inverse[0, 0, 0:1, :] + down0 * inverse[1, 0, 0:1, :] * up0
    return up1 * up0, response, down0 * down1


def group_response(load, inverse, vertical):
    link0, link1 = vertical[7:8, :], vertical[15:16, :]
    down0 = link0 * inverse[0, 0, 7:8, :]
    last0 = first0 = last1 = first1 = None
    for j in range(8):
        value0, value1 = load(j), load(8 + j)
        terms = (
            inverse[0, 7, j : j + 1, :] * value0,
            inverse[0, 0, j : j + 1, :] * value0,
            inverse[1, 7, j : j + 1, :] * value1,
            inverse[1, 0, j : j + 1, :] * value1,
        )
        if j == 0:
            last0, first0, last1, first1 = terms
        else:
            last0, first0, last1, first1 = (
                last0 + terms[0],
                first0 + terms[1],
                last1 + terms[2],
                first1 + terms[3],
            )
    carried = link0 * last0
    upward = link1 * (last1 + inverse[1, 7, 0:1, :] * carried)
    downward = first0 + down0 * (first1 + inverse[1, 0, 0:1, :] * carried)
    return upward, downward


def total_of(values):
    return jnp.sum(jnp.sum(values, axis=1, keepdims=True), axis=0, keepdims=True)


def begin_kernel(count, right_side, inverse, vertical, residual, message):
    tile = pl.program_id(0)
    lanes = lax.broadcasted_iota(jnp.int32, (NODES, LANES), 1)
    living = lanes + tile * LANES < count[0]

    for level in range(LEVELS):
        residual[level] = jnp.where(living, right_side[level], 0.0)
    upward, downward = group_response(lambda level: residual[level], inverse, vertical)
    message[0, 0:16, :] = upward
    message[0, 16:32, :] = downward
    coupling = group_rows(inverse, vertical)
    for row in range(3):
        message[0, 32 + row : 33 + row, :] = coupling[row]
    link = vertical[15:16, :]
    message[0, 35:36, :] = link * (link * inverse[1, 7, 7:8, :] - 1.0)
    message[0, 36:40, :] = jnp.zeros((4, LANES), F32)


def joined(first, last, *refs):
    refs = list(refs)
    flags, seg, got, inner = refs[:4]
    del refs[:4]
    if first:
        aux = refs.pop(0)
    else:
        terms = refs.pop(0)
    if last:
        own = refs.pop(0)
        if not first:
            ends = refs.pop(0)
        carried = refs.pop(0)
    else:
        seg_out, inner_out = refs.pop(0), refs.pop(0)
    if first:
        terms, aux_out = refs.pop(0), refs.pop(0)
        if last:
            ends = refs.pop(0)

    def row(ref, tile, index):
        return ref[tile, index : index + 1, :]

    def finish(tile, below, above_up, above_down):
        if last:
            leaving = row(ends, tile, 1) * below + own[tile, 0:16, :]
            carried[tile, 0:16, :] = below
            carried[tile, 16:32, :] = above_down + row(ends, tile, 0) * leaving
        else:
            inner_out[tile, 0:16, :] = below
            inner_out[tile, 16:32, :] = above_up
            inner_out[tile, 32:48, :] = above_down

    def prepare(tile, partner_below):
        for index in range(3):
            terms[tile, index : index + 1, :] = row(got, tile, 32 + index)
            terms[tile, 3 + index : 4 + index, :] = row(seg, tile, 32 + index)
        terms[tile, 6:7, :] = row(aux, tile, 0)
        terms[tile, 7:8, :] = row(aux, tile, 3)
        up_p, both_p, down_p, up, both, down = [row(terms, tile, index) for index in range(6)]
        below, above, through, back, flow = [row(aux, tile, index) for index in range(5)]
        if partner_below:
            bottom = jnp.broadcast_to(flags[1], flow.shape)
            flow = jnp.where(bottom == 1, row(got, tile, 35), flow)
            below = below * up_p
            joint = (up * up_p, both_p + down_p * both * up_p, down_p * down, row(seg, tile, 35))
        else:
            through = through + back * both_p * above
            above = up_p * above
            back = back * down_p
            joint = (up_p * up, both + down * both_p * up, down * down_p, row(got, tile, 35))
        for index, value in enumerate((below, above, through, back, flow)):
            aux_out[tile, index : index + 1, :] = value
        aux_out[tile, 5:8, :] = jnp.zeros((3, LANES), F32)
        if last:
            ends[tile, 0:1, :] = through
            ends[tile, 1:2, :] = row(own, tile, 32)
            ends[tile, 2:8, :] = jnp.zeros((6, LANES), F32)
        else:
            for index, value in enumerate(joint):
                seg_out[tile, 32 + index : 33 + index, :] = value
            seg_out[tile, 36:40, :] = jnp.zeros((4, LANES), F32)

    @pl.when(flags[0] == 1)
    def partner_below():
        for tile in range(GROUPS):
            if first:
                prepare(tile, True)
            came_up, came_down = got[tile, 0:16, :], got[tile, 16:32, :]
            if not last:
                upward, downward = seg[tile, 0:16, :], seg[tile, 16:32, :]
                seg_out[tile, 0:16, :] = row(terms, tile, 3) * came_up + upward
                seg_out[tile, 16:32, :] = came_down + row(terms, tile, 2) * (
                    downward + row(terms, tile, 4) * came_up
                )
            below = row(terms, tile, 6) * came_up + inner[tile, 0:16, :]
            finish(tile, below, inner[tile, 16:32, :], inner[tile, 32:48, :])

    @pl.when(flags[0] != 1)
    def partner_above():
        for tile in range(GROUPS):
            if first:
                prepare(tile, False)
            came_up, came_down = got[tile, 0:16, :], got[tile, 16:32, :]
            if not last:
                upward, downward = seg[tile, 0:16, :], seg[tile, 16:32, :]
                seg_out[tile, 0:16, :] = row(terms, tile, 0) * upward + came_up
                seg_out[tile, 16:32, :] = downward + row(terms, tile, 5) * (
                    came_down + row(terms, tile, 1) * upward
                )
            above_up, above_down = inner[tile, 16:32, :], inner[tile, 32:48, :]
            finish(
                tile,
                inner[tile, 0:16, :],
                row(terms, tile, 0) * above_up + came_up,
                above_down + row(terms, tile, 7) * (came_down + row(terms, tile, 1) * above_up),
            )


def solve_kernel(stage, last, *refs):
    refs = list(refs)

    def take(count):
        taken = refs[:count]
        del refs[:count]
        return taken

    count, inverse, vertical, residual_in, came = take(5)
    if stage:
        smoothed_in, applied, state_in = take(3)
        dot_parts = take(2)
    if stage == 2:
        solution_in, direction_in, image_in, flow_in, scalars_in = take(5)
    if stage:
        solution, residual, direction, scalars_out = take(4)
        if not last:
            image, flow, state = take(3)
    else:
        residual, state = residual_in, came
    smoothed, product = take(2)
    if not last:
        near, far, tables = take(3)
    (parts,) = take(1)
    tile = pl.program_id(0)
    rows, lanes = iotas()

    if stage:
        dots = dot_parts[0][...] + dot_parts[1][...]
        norm = jnp.sum(dots[0:1, :], axis=1, keepdims=True)
        curvature = jnp.sum(dots[1:2, :], axis=1, keepdims=True)
        if stage == 2:
            cross = jnp.sum(dots[2:3, :], axis=1, keepdims=True)
            ratio = norm / scalars_in[0:1, 0:1]
            curvature = curvature + ratio * cross + ratio * ratio * scalars_in[1:2, 0:1]
        step_size = norm / curvature
        scalars_out[0:1, :] = jnp.broadcast_to(norm, (1, LANES))
        scalars_out[1:2, :] = jnp.broadcast_to(curvature, (1, LANES))
        scalars_out[2:8, :] = jnp.zeros((6, LANES), F32)
        for level in range(LEVELS):
            value = smoothed_in[level]
            result = applied[level]
            if stage == 2:
                value = value + ratio * direction_in[level]
                result = result + ratio * image_in[level]
                solution[level] = solution_in[level] + step_size * value
            else:
                solution[level] = step_size * value
            direction[level] = value
            if not last:
                image[level] = result
            residual[level] = residual_in[level] - step_size * result
        change = came[0, 0:32, :]
        if stage == 2:
            change = change + ratio * flow_in[0]
        incoming = state_in[0, 0:32, :] - step_size * change
        if not last:
            flow[0] = change
            state[0] = incoming
    else:
        incoming = came[0, 0:32, :]
    link0, link1 = vertical[7:8, :], vertical[15:16, :]
    below = incoming[0:16]
    above = incoming[16:32]

    def block_product(block, lifted):
        solved = []
        for i in range(8):
            total = inverse[block, i, 0:1, :] * lifted[0]
            for j in range(1, 8):
                total = total + inverse[block, i, j : j + 1, :] * lifted[j]
            solved.append(total)
        return solved

    values = [residual[level] for level in range(8)]
    lower = block_product(0, [values[0] + below] + values[1:])
    values = [residual[8 + level] for level in range(8)]
    upper = block_product(1, [values[0] + link0 * lower[7]] + values[1:])
    lift = link1 * above
    upper = [upper[i] + lift * inverse[1, i, 7:8, :] for i in range(8)]
    lift = link0 * upper[0]
    lower = [lower[i] + lift * inverse[0, i, 7:8, :] for i in range(8)]
    total = None
    for level, value in enumerate(lower + upper):
        smoothed[level] = value
        term = value * residual[level]
        total = term if total is None else total + term

    @pl.when(tile == 0)
    def clear():
        parts[...] = jnp.zeros((16, LANES), F32)

    parts[...] += total

    @pl.when(tile == GROUPS - 1)
    def finish():
        product[...] = jnp.broadcast_to(jnp.sum(parts[...], axis=0, keepdims=True), product.shape)

    if last:
        return

    start = count[0] - LANES
    start_tile = lax.shift_right_logical(start, 7)
    offset = jnp.bitwise_and(start, LANES - 1)
    extra = start - 1
    extra_tile = lax.shift_right_logical(extra, 7)
    extra_lane = jnp.bitwise_and(extra, LANES - 1)
    in_tail = (tile == start_tile) | (tile == start_tile + 1)
    in_extra = tile == extra_tile

    def put(position, value):
        tables[position] = value

    @pl.when(in_tail | in_extra | (tile < 2))
    def build():
        store_tables(lambda level: smoothed[level], rows, put)

    def fill(tail, head):
        @pl.when(tile == 0)
        def clear_tail():
            tail[...] = jnp.zeros((25, 8, LANES), F32)
            head[...] = jnp.zeros((25, 8, LANES), F32)

        @pl.when(in_tail)
        def fill_tail():
            index = jnp.bitwise_and(lanes + offset, LANES - 1)
            before_wrap = (lanes < LANES - offset).astype(jnp.int32)
            wanted = before_wrap == (tile == start_tile).astype(jnp.int32)
            for position in range(24):
                tail[position] = jnp.where(
                    wanted, lane_take(tables[position], index), tail[position]
                )

        @pl.when(in_extra)
        def fill_extra():
            index = jnp.zeros_like(lanes) + extra_lane
            packed = jnp.zeros((8, LANES), F32)
            for position in range(24):
                packed = jnp.where(lanes == position, lane_take(tables[position], index), packed)
            tail[24] = packed

        @pl.when(tile == 0)
        def fill_head():
            for position in range(24):
                head[position] = tables[position]

        @pl.when(tile == 1)
        def fill_head_extra():
            packed = jnp.zeros((8, LANES), F32)
            for position in range(24):
                packed = jnp.where(
                    lanes == position, lane_take(tables[position], jnp.zeros_like(lanes)), packed
                )
            head[24] = packed

    odd = jnp.bitwise_and(count[1], 1)
    pl.when(odd == 0)(lambda: fill(near, far))
    pl.when(odd == 1)(lambda: fill(far, near))


def finish_kernel(norms, scalars_in, smoothed, direction_in, direction):
    ratio = total_of(norms[...]) / scalars_in[0:1, 0:1]
    for level in range(LEVELS):
        direction[level] = smoothed[level] + ratio * direction_in[level]


def split(values):
    high = values.astype(BF16)
    return high, (values - high.astype(F32)).astype(BF16)


def product3(tables, rows, columns, values):
    high, low = split(values)
    result = jnp.dot(tables[0, rows, columns], high, preferred_element_type=F32)
    result = result + jnp.dot(tables[0, rows, columns], low, preferred_element_type=F32)
    return result + jnp.dot(tables[1, rows, columns], high, preferred_element_type=F32)


def operate_kernel(
    helmholtz,
    plan,
    field,
    ints,
    copies,
    metric,
    mass,
    vertical,
    below_row,
    state,
    tables,
    applied,
    table,
    edges,
    corners,
    pick,
):
    tile = pl.program_id(0)
    rows, lanes = iotas()
    here = pl.ds(pl.multiple_of(tile * LANES, LANES), LANES)

    @pl.when(tile == 0)
    def build():
        def one(part, unused):
            there = pl.ds(pl.multiple_of(part * LANES, LANES), LANES)

            def put(position, value):
                table[position, :, there] = value

            store_tables(lambda level: field[level, :, there], rows, put)
            return unused

        lax.fori_loop(0, GROUPS, one, 0)

    gather_pick(table, 0, ints, plan, False, tile, edges, corners, pick)
    mixed, along_y, along_x = metric[1], metric[2], metric[0]
    for half in range(2):
        values = jnp.concatenate([field[8 * half + level, :, here] for level in range(8)], axis=0)
        gradients = product3(tables, slice(0, 256), slice(0, 128), values)
        flux_x = []
        flux_y = []
        for level in range(8):
            part_x = gradients[16 * level : 16 * level + 16]
            part_y = gradients[128 + 16 * level : 144 + 16 * level]
            flux_x.append(along_x * part_x + mixed * part_y)
            flux_y.append(mixed * part_x + along_y * part_y)
        stiff = product3(tables, slice(256, 384), slice(0, 256), jnp.concatenate(flux_x + flux_y, axis=0))
        for level in range(8):
            applied[8 * half + level] = stiff[16 * level : 16 * level + 16]
    twice = PENALTY * copies[...]
    flux = state[0, 0:16, :] + below_row[0, 4:5, :] * field[0, :, here]
    for level in range(LEVELS):
        value = field[level, :, here]
        higher = field[level + 1, :, here] if level < LEVELS - 1 else state[0, 16:32, :]
        next_flux = vertical[level : level + 1, :] * (value - higher)
        applied[level] = (
            applied[level]
            + (helmholtz[level] * mass[...] + twice) * value
            + (next_flux - flux)
            - PENALTY * pick[level]
        )
        flux = next_flux


def image_kernel(first, *refs):
    count, plan, applied, smoothed, ints, near, far, product, inverse, vertical = refs[:10]
    refs = refs[10:]
    if not first:
        direction, previous = refs[:2]
        refs = refs[2:]
    image, message, dots, table, edges, corners, pick, parts, crosses = refs
    tile = pl.program_id(0)
    rows, lanes = iotas()

    @pl.when(tile == 0)
    def build():
        parts[...] = jnp.zeros((16, LANES), F32)
        crosses[...] = jnp.zeros((16, LANES), F32)

        def fill(before, after):
            for position in range(24):
                index = jnp.full((8, LANES), position, jnp.int32)
                table[position, :, 0:LANES] = before[position]
                table[position, :, LANES : 2 * LANES] = after[position]
                table[position, :, 2 * LANES : 3 * LANES] = jnp.where(
                    lanes == 0, lane_take(before[24], index), lane_take(after[24], index)
                )

        odd = jnp.bitwise_and(count[1], 1)
        pl.when(odd == 0)(lambda: fill(far, near))
        pl.when(odd == 1)(lambda: fill(near, far))

    pick[...] = jnp.zeros((LEVELS, NODES, LANES), F32)

    @pl.when(plan[tile * PLAN + 1] > 0)
    def reach():
        gather_pick(table, 8, ints, plan, True, tile, edges, corners, pick)

    total = cross = None
    for level in range(LEVELS):
        value = smoothed[level]
        result = applied[level] - PENALTY * pick[level]
        image[level] = result
        term = value * result
        total = term if total is None else total + term
        if not first:
            term = value * previous[level] + direction[level] * result
            cross = term if cross is None else cross + term
    parts[...] += total
    if not first:
        crosses[...] += cross
    upward, downward = group_response(lambda level: image[level], inverse, vertical)
    message[0, 0:16, :] = upward
    message[0, 16:32, :] = downward

    @pl.when(tile == GROUPS - 1)
    def finish():
        dots[0:1, :] = product[0:1, :]
        dots[1:2, :] = jnp.sum(parts[...], axis=0, keepdims=True)
        dots[2:3, :] = jnp.sum(crosses[...], axis=0, keepdims=True)
        dots[3:8, :] = jnp.zeros((5, LANES), F32)


def field_spec():
    return pl.BlockSpec((LEVELS, NODES, LANES), lambda t: (0, 0, t))


def row_spec(rows):
    return pl.BlockSpec((rows, LANES), lambda t: (0, t))


def whole(*shape):
    return pl.BlockSpec(shape, lambda t: (0,) * len(shape))


def tile_spec(rows):
    return pl.BlockSpec((1, rows, LANES), lambda t: (t, 0, 0))


def inverse_spec():
    return pl.BlockSpec((2, 8, 8, LANES), lambda t: (0, 0, 0, t))


def scalars():
    return pl.BlockSpec(memory_space=pltpu.SMEM)


def struct(*shape):
    return jax.ShapeDtypeStruct(shape, F32)


def call(kernel, name, in_specs, out_specs, out_shape, scratch, cost, args):
    return pl.pallas_call(
        kernel,
        grid=(GROUPS,),
        in_specs=in_specs,
        out_specs=out_specs,
        out_shape=out_shape,
        scratch_shapes=scratch,
        name=name,
        compiler_params=pltpu.CompilerParams(
            dimension_semantics=("arbitrary",), vmem_limit_bytes=VMEM_BYTES
        ),
        cost_estimate=pl.CostEstimate(flops=cost, bytes_accessed=6 << 20, transcendentals=0),
    )(*args)


FIELD = (LEVELS, NODES, 1024)
PICK_SCRATCH = [
    ((4, LEVELS, 8, LANES), F32),
    ((4, 8, 8, LANES), F32),
    ((LEVELS, NODES, LANES), F32),
]


def vmem(shapes):
    return [pltpu.VMEM(shape, dtype) for shape, dtype in shapes]


def prepare_kernel(place, edge_rows, flip_rows, corner_rows, ints, copies):
    position, count_before = place[0], place[1]

    def source_of(entry):
        element = lax.shift_right_logical(entry, 2)
        holder = lax.shift_right_logical(element, 10)
        within = jnp.bitwise_and(element, 1023)
        earlier = within - (count_before - BORDER)
        earlier = jnp.where(earlier == 0, 10 * LANES, 8 * LANES + earlier - 1)
        later = jnp.where(within < LANES, 9 * LANES + within, 10 * LANES + 1)
        source = jnp.where(holder == position, within, jnp.where(holder < position, earlier, later))
        return jnp.where(entry >= 0, source, ABSENT)

    edges, corners = edge_rows[...], corner_rows[...]
    ints[0:4, :] = source_of(edges)
    ints[4:16, :] = source_of(corners)
    flipped = (flip_rows[...] == 1).astype(jnp.int32)
    straight = 2 * jnp.bitwise_and(edges, 3) + flipped
    swapped_row = 2 * jnp.bitwise_and(edges, 3) + 1 - flipped
    none = jnp.zeros((1, LANES), jnp.int32)

    def of(rows, side):
        return rows[side : side + 1, :]

    low = [none, of(straight, 0), of(swapped_row, 0), none, of(straight, 3), none, none, of(straight, 1)]
    high = [of(swapped_row, 3), none, none, of(swapped_row, 1), none, of(straight, 2),
            of(swapped_row, 2), none]
    for row, value in enumerate(low + high):
        ints[16 + row : 17 + row, :] = value
    ints[32:36, :] = jnp.zeros((4, LANES), jnp.int32)
    ints[36:48, :] = jnp.bitwise_and(corners, 3)
    on = (edges >= 0).astype(F32)
    there = (corners >= 0).astype(F32)
    shared = [
        of(there, 3 * corner) + of(there, 3 * corner + 1) + of(there, 3 * corner + 2)
        for corner in range(4)
    ]
    zero = jnp.zeros((1, LANES), F32)
    rows = [
        shared[0], of(on, 0), of(on, 0), shared[1], of(on, 3), zero, zero, of(on, 1),
        of(on, 3), zero, zero, of(on, 1), shared[3], of(on, 2), of(on, 2), shared[2],
    ]
    for row, value in enumerate(rows):
        copies[row : row + 1, :] = value


def gather_plan(ints):
    holder = (ints[:16] // LANES).reshape(16, 8, LANES)
    tiles = jnp.arange(11, dtype=jnp.int32)
    by_item = jnp.any(holder[:, :, None, :] == tiles[None, None, :, None], axis=3)
    used = jnp.any(by_item, axis=0)
    entry = tiles[None] + 16 * jnp.any(by_item[:4], axis=0).astype(jnp.int32)
    far = tiles >= 8
    same = far[:, None] == far[None, :]
    earlier = used[:, None, :] & (same & (tiles[None, :] < tiles[:, None]))[None]
    place = jnp.sum(earlier.astype(jnp.int32), axis=2) + jnp.where(far, 10, 2)[None]
    columns = jnp.arange(PLAN, dtype=jnp.int32)
    listed = (place[:, :, None] == columns) * entry[:, :, None]
    counted = columns[None, :] == jnp.where(far, 1, 0)[:, None]
    values = jnp.where(used[:, :, None], listed + counted[None].astype(jnp.int32), 0)
    return jnp.sum(values, axis=1).astype(jnp.int32).reshape(-1)


def parts_along(value, peers, inner):
    side = math.isqrt(peers)
    parts = []
    for shift in range(1, side):
        pairs = []
        for i in range(peers):
            outer, within = i // side, i % side
            if inner:
                pairs.append((i, outer * side + (within ^ shift)))
            else:
                pairs.append((i, (outer ^ shift) * side + within))
        parts.append(lax.ppermute(value, "elem", pairs))
    return parts


def swapped(value, distance):
    return lax.ppermute(value, "lev", [(i, i ^ distance) for i in range(GROUPS)])


def join(name, first, last, shapes, args):
    return pl.pallas_call(
        lambda *refs: joined(first, last, *refs),
        in_specs=[scalars()] + [pl.BlockSpec(memory_space=pltpu.VMEM)] * (len(args) - 1),
        out_shape=[struct(8, rows, LANES) for rows in shapes],
        name=name,
        cost_estimate=pl.CostEstimate(flops=1 << 16, bytes_accessed=1 << 18, transcendentals=0),
        compiler_params=pltpu.CompilerParams(vmem_limit_bytes=SMALL_VMEM_BYTES),
    )(*args)


def body(
    right_side,
    metric,
    mass_weight,
    helmholtz,
    vertical,
    block_inverse,
    edge_neighbour,
    edge_flip,
    corner_neighbour,
    element_count,
):
    peers = lax.axis_size("elem")
    position = lax.axis_index("elem")
    upward_elem = [(i, i + 1) for i in range(peers - 1)]
    near_pairs = [(i, i ^ 1) for i in range(peers)]
    far_pairs = [(i, i - 1 if i % 2 == 0 else i + 1) for i in range(1, peers - 1)]
    count = jnp.concatenate([element_count, position.astype(jnp.int32)[None]])

    residual, message = call(
        begin_kernel,
        "begin",
        [scalars(), field_spec(), inverse_spec(), row_spec(16)],
        [field_spec(), tile_spec(40)],
        [struct(*FIELD), struct(8, 40, LANES)],
        [],
        1 << 22,
        (element_count, right_side, block_inverse, vertical),
    )
    group = lax.axis_index("lev")
    flags = [
        jnp.stack([(group >> step) & 1, ((group & (2**step - 1)) == 0).astype(jnp.int32)])
        for step in range(3)
    ]
    ones = jnp.ones((8, 1, LANES), F32)
    nothing = jnp.zeros((8, 1, LANES), F32)
    aux = jnp.concatenate([ones, ones, nothing, ones] + [nothing] * 4, axis=1)
    empty = jnp.zeros((8, 48, LANES), F32)
    terms = [None] * 3
    seg, inner = message, empty
    for step in range(2):
        got = swapped(seg, 2**step)
        seg, inner, terms[step], aux = join(
            "join_first", True, False, [40, 48, 8, 8], (flags[step], seg, got, inner, aux)
        )
    got = swapped(seg, 4)
    came, terms[2], below_row, ends = join(
        "join_first_last", True, True, [32, 8, 8, 8], (flags[2], seg, got, inner, aux, message)
    )

    count_before = lax.ppermute(element_count, "elem", upward_elem)[0]
    ints, copies = call(
        prepare_kernel,
        "prepare",
        [scalars(), row_spec(4), row_spec(4), row_spec(12)],
        [row_spec(48), row_spec(16)],
        [jax.ShapeDtypeStruct((48, 1024), jnp.int32), struct(16, 1024)],
        [],
        1 << 18,
        (
            jnp.stack([position, count_before]).astype(jnp.int32),
            jnp.transpose(edge_neighbour),
            jnp.transpose(edge_flip),
            jnp.transpose(corner_neighbour, (1, 2, 0)).reshape(12, 1024),
        ),
    )
    plan = gather_plan(ints)
    tables = stacked_tables()

    shared_specs = [scalars(), inverse_spec(), row_spec(16), field_spec(), tile_spec(32)]
    halo = struct(25, 8, LANES)
    smoothed, product, near, far = call(
        lambda *refs: solve_kernel(0, False, *refs),
        "solve_first",
        shared_specs,
        [field_spec(), whole(8, LANES), whole(25, 8, LANES), whole(25, 8, LANES)],
        [struct(*FIELD), struct(8, LANES), halo, halo],
        vmem([((24, 8, LANES), F32), ((16, LANES), F32)]),
        1 << 22,
        (count, block_inverse, vertical, residual, came),
    )
    state = came
    solution = direction = image = flow = scalar_rows = None
    for iteration in range(ITERATIONS):
        first = iteration == 0
        last = iteration == ITERATIONS - 1
        near = lax.ppermute(near, "elem", near_pairs)
        far = lax.ppermute(far, "elem", far_pairs)
        applied = call(
            operate_kernel,
            "operate",
            [
                scalars(), scalars(), whole(*FIELD), row_spec(48), row_spec(16),
                pl.BlockSpec((3, NODES, LANES), lambda t: (0, 0, t)), row_spec(16), row_spec(16),
                tile_spec(8), tile_spec(32), whole(2, 384, 256),
            ],
            field_spec(),
            struct(*FIELD),
            vmem([((24, 8, 1024), F32)] + PICK_SCRATCH),
            1 << 30,
            (
                helmholtz, plan, smoothed, ints, copies, metric, mass_weight,
                vertical, below_row, state, tables,
            ),
        )
        args = [
            count, plan, applied, smoothed, ints, near, far, product, block_inverse,
            vertical,
        ]
        specs = [
            scalars(), scalars(), field_spec(), field_spec(), row_spec(48), whole(25, 8, LANES),
            whole(25, 8, LANES), whole(8, LANES), inverse_spec(), row_spec(16),
        ]
        if not first:
            args += [direction, image]
            specs += [field_spec(), field_spec()]
        applied, message, dots = call(
            lambda *refs, first=first: image_kernel(first, *refs),
            "image_first" if first else "image",
            specs,
            [field_spec(), tile_spec(32), whole(8, LANES)],
            [struct(*FIELD), struct(8, 32, LANES), struct(8, LANES)],
            vmem(
                [((24, 8, 3 * LANES), F32)] + PICK_SCRATCH + [((16, LANES), F32), ((16, LANES), F32)]
            ),
            1 << 22,
            args,
        )
        seg, inner = message, empty
        for step in range(2):
            got = swapped(seg, 2**step)
            others = parts_along(dots, peers, step == 0)
            got, *others = lax.optimization_barrier((got, *others))
            dots = (dots + others[0]) + (others[1] + others[2])
            seg, inner = join(
                "join", False, False, [32, 48], (flags[step], seg, got, inner, terms[step])
            )
        got = swapped(seg, 4)
        other = swapped(dots, 4)
        got, other = lax.optimization_barrier((got, other))
        dots = dots + other
        (came,) = join(
            "join_last", False, True, [32], (flags[2], seg, got, inner, terms[2], message, ends)
        )
        dots = dots + swapped(dots, 2)
        dots = [dots, swapped(dots, 1)]

        args = [count, block_inverse, vertical, residual, came, smoothed, applied, state] + dots
        specs = shared_specs + [field_spec(), field_spec(), tile_spec(32)] + [whole(8, LANES)] * 2
        if not first:
            args += [solution, direction, image, flow, scalar_rows]
            specs += [field_spec(), field_spec(), field_spec(), tile_spec(32), whole(8, LANES)]
        out_specs = [field_spec(), field_spec(), field_spec(), whole(8, LANES)]
        shapes = [struct(*FIELD), struct(*FIELD), struct(*FIELD), struct(8, LANES)]
        if last:
            out_specs += [field_spec(), whole(LANES, LANES)]
            shapes += [struct(*FIELD), struct(LANES, LANES)]
            scratch = vmem([((16, LANES), F32)])
        else:
            out_specs += [field_spec(), tile_spec(32), tile_spec(32), field_spec(), whole(8, LANES)]
            out_specs += [whole(25, 8, LANES), whole(25, 8, LANES)]
            shapes += [struct(*FIELD), struct(8, 32, LANES), struct(8, 32, LANES), struct(*FIELD)]
            shapes += [struct(8, LANES), halo, halo]
            scratch = vmem([((24, 8, LANES), F32), ((16, LANES), F32)])
        results = call(
            lambda *refs, first=first, last=last: solve_kernel(1 if first else 2, last, *refs),
            "solve_last" if last else "solve",
            specs,
            out_specs,
            shapes,
            scratch,
            1 << 22,
            args,
        )
        if last:
            solution, residual, direction, scalar_rows, smoothed, product = results
        else:
            solution, residual, direction, scalar_rows, image, flow, state = results[:7]
            smoothed, product, near, far = results[7:]
    norms = lax.all_to_all(product, ("elem", "lev"), split_axis=0, concat_axis=0, tiled=True)
    direction = call(
        finish_kernel,
        "finish",
        [whole(LANES, LANES), whole(8, LANES), field_spec(), field_spec()],
        field_spec(),
        struct(*FIELD),
        [],
        1 << 20,
        (norms, scalar_rows, smoothed, direction),
    )
    return (solution, residual, direction)


def solution(mesh):
    in_specs = (
        P("lev", None, "elem"),
        P(None, None, "elem"),
        P(None, "elem"),
        P("lev"),
        P("lev", "elem"),
        P("lev", None, None, "elem"),
        P("elem", None),
        P("elem", None),
        P("elem", None, None),
        P("elem"),
    )
    out_specs = (P("lev", None, "elem"), P("lev", None, "elem"), P("lev", None, "elem"))
    return jax.shard_map(body, mesh=mesh, in_specs=in_specs, out_specs=out_specs, check_vma=False)
```

```python
import math

import jax
import jax.numpy as jnp
import numpy as np
from jax import lax
from jax.experimental import pallas as pl
from jax.experimental.pallas import tpu as pltpu
from jax.sharding import PartitionSpec as P

COLUMNS = 128
ITERATIONS = 3
BORDER = COLUMNS + 1
LANES = 128
LEVELS = 16
NODES = 16
GROUPS = 8
PENALTY = 2.0
ABSENT = 15 * LANES
PLAN = 13
VMEM_BYTES = 12 * 1024 * 1024
SMALL_VMEM_BYTES = 4 * 1024 * 1024
F32 = jnp.float32
BF16 = jnp.bfloat16


def gradient_table():
    root = 1.0 / math.sqrt(5.0)
    points = [-1.0, -root, root, 1.0]
    legendre = [0.5 * (5.0 * p * p * p - 3.0 * p) for p in points]
    matrix = [[0.0 for col in range(4)] for row in range(4)]
    for row in range(4):
        for col in range(4):
            if row != col:
                matrix[row][col] = legendre[row] / (legendre[col] * (points[row] - points[col]))
    matrix[0][0] = -3.0
    matrix[3][3] = 3.0
    derivative = np.array(matrix)
    return np.kron(np.eye(4), derivative), np.kron(derivative, np.eye(4))


def stacked_tables():
    along_x, along_y = gradient_table()
    table = np.concatenate([np.kron(np.eye(8), along_x), np.kron(np.eye(8), along_y)], axis=0)
    both = np.zeros((384, 256))
    both[:256, :128] = table
    both[256:] = table.T
    both = jnp.asarray(both, F32)
    high = both.astype(BF16)
    return jnp.stack([high, (both - high.astype(F32)).astype(BF16)])


def lane_take(values, index):
    return jnp.take_along_axis(values, index, axis=1, mode="promise_in_bounds")


def row_take(values, index):
    return jnp.take_along_axis(values, index, axis=0, mode="promise_in_bounds")


def iotas():
    rows = lax.broadcasted_iota(jnp.int32, (8, LANES), 0)
    lanes = lax.broadcasted_iota(jnp.int32, (8, LANES), 1)
    return rows, lanes


def by_row(rows, values):
    index = jnp.zeros_like(rows)
    for row, value in enumerate(values):
        if value:
            index = jnp.where(rows == row, value, index)
    return index


def edge_table(low, high, rows):
    from_low = row_take(low, by_row(rows, [1, 2, 7, 0, 0, 0, 4, 0]))
    from_high = row_take(high, by_row(rows, [0, 0, 0, 3, 5, 6, 0, 0]))
    use_low = (rows < 3) | (rows == 6)
    return jnp.where(use_low, from_low, from_high)


def corner_table(low, high, low_next, high_next, rows):
    index_low = by_row(rows, [0, 3, 0, 0, 0, 3, 0, 0])
    index_high = by_row(rows, [0, 0, 7, 4, 0, 0, 7, 4])
    first = jnp.where(rows < 2, row_take(low, index_low), row_take(high, index_high))
    second = jnp.where(rows < 6, row_take(low_next, index_low), row_take(high_next, index_high))
    return jnp.where(rows < 4, first, second)


def store_tables(load, rows, put):
    for pair in range(LEVELS // 2):
        even = load(2 * pair)
        odd = load(2 * pair + 1)
        put(2 * pair, edge_table(even[:8], even[8:], rows))
        put(2 * pair + 1, edge_table(odd[:8], odd[8:], rows))
        put(LEVELS + pair, corner_table(even[:8], even[8:], odd[:8], odd[8:], rows))


def gather_pick(table, first_tile, ints, plan, far, tile, edges, corners, pick):
    rows, lanes = iotas()
    edges[...] = jnp.zeros(edges.shape, F32)
    corners[...] = jnp.zeros(corners.shape, F32)

    def step(turn, unused):
        which = plan[tile * PLAN + (10 if far else 2) + turn]
        column = pl.multiple_of((which - first_tile) * LANES, LANES)
        values = [table[member, :, pl.ds(column, LANES)] for member in range(LEVELS + 8)]
        for side in range(4):
            source = jnp.broadcast_to(ints[side : side + 1, :], (8, LANES))
            lane = jnp.bitwise_and(source, LANES - 1)
            hit = lax.shift_right_logical(source, 7) == which
            for place in range(LEVELS):
                edges[side, place] = jnp.where(
                    hit, lane_take(values[place], lane), edges[side, place]
                )
        for corner in range(4):
            sums = [corners[corner, place] for place in range(8)]
            for other in range(3):
                item = 4 + 3 * corner + other
                source = jnp.broadcast_to(ints[item : item + 1, :], (8, LANES))
                node = jnp.broadcast_to(ints[32 + item : 33 + item, :], (8, LANES))
                lane = jnp.bitwise_and(source, LANES - 1)
                hit = (lax.shift_right_logical(source, 7) == which) & (
                    jnp.bitwise_and(rows, 3) == node
                )
                for place in range(8):
                    sums[place] = sums[place] + jnp.where(
                        hit, lane_take(values[LEVELS + place], lane), 0.0
                    )
            for place in range(8):
                corners[corner, place] = sums[place]
        return unused

    lax.fori_loop(0, plan[tile * PLAN + (1 if far else 0)], step, 0)
    low_index = ints[16:24, :]
    high_index = ints[24:32, :]
    for pair in range(LEVELS // 2):
        sums = []
        for corner in range(4):
            total = corners[corner, pair]
            near, far_by = (7, 6) if corner in (0, 3) else (1, 2)
            total = total + pltpu.roll(total, near, 0)
            total = total + pltpu.roll(total, far_by, 0)
            sums.append((total, pltpu.roll(total, 4, 0)))
        for half in range(2):
            level = 2 * pair + half
            low = jnp.where(
                (rows == 1) | (rows == 2),
                row_take(edges[0, level], low_index),
                jnp.where(
                    rows == 7,
                    row_take(edges[1, level], low_index),
                    row_take(edges[3, level], low_index),
                ),
            )
            low = jnp.where((rows == 5) | (rows == 6), 0.0, low)
            high = jnp.where(
                rows == 3,
                row_take(edges[1, level], high_index),
                jnp.where(
                    rows == 0,
                    row_take(edges[3, level], high_index),
                    row_take(edges[2, level], high_index),
                ),
            )
            high = jnp.where((rows == 1) | (rows == 2), 0.0, high)
            low = jnp.where(rows == 0, sums[0][half], jnp.where(rows == 3, sums[1][half], low))
            high = jnp.where(rows == 7, sums[2][1 - half], jnp.where(rows == 4, sums[3][1 - half], high))
            pick[level, 0:8, :] = low
            pick[level, 8:16, :] = high


def group_rows(inverse, vertical):
    link0, link1 = vertical[7:8, :], vertical[15:16, :]
    up0 = link0 * inverse[0, 7, 0:1, :]
    up1 = link1 * inverse[1, 7, 0:1, :]
    down0 = link0 * inverse[0, 0, 7:8, :]
    down1 = link1 * inverse[1, 0, 7:8, :]
    response = inverse[0, 0, 0:1, :] + down0 * inverse[1, 0, 0:1, :] * up0
    return up1 * up0, response, down0 * down1


def group_response(load, inverse, vertical):
    link0, link1 = vertical[7:8, :], vertical[15:16, :]
    down0 = link0 * inverse[0, 0, 7:8, :]
    last0 = first0 = last1 = first1 = None
    for j in range(8):
        value0, value1 = load(j), load(8 + j)
        terms = (
            inverse[0, 7, j : j + 1, :] * value0,
            inverse[0, 0, j : j + 1, :] * value0,
            inverse[1, 7, j : j + 1, :] * value1,
            inverse[1, 0, j : j + 1, :] * value1,
        )
        if j == 0:
            last0, first0, last1, first1 = terms
        else:
            last0, first0, last1, first1 = (
                last0 + terms[0],
                first0 + terms[1],
                last1 + terms[2],
                first1 + terms[3],
            )
    carried = link0 * last0
    upward = link1 * (last1 + inverse[1, 7, 0:1, :] * carried)
    downward = first0 + down0 * (first1 + inverse[1, 0, 0:1, :] * carried)
    return upward, downward


def total_of(values):
    return jnp.sum(jnp.sum(values, axis=1, keepdims=True), axis=0, keepdims=True)


def begin_kernel(count, right_side, inverse, vertical, residual, message):
    tile = pl.program_id(0)
    lanes = lax.broadcasted_iota(jnp.int32, (NODES, LANES), 1)
    living = lanes + tile * LANES < count[0]

    for level in range(LEVELS):
        residual[level] = jnp.where(living, right_side[level], 0.0)
    upward, downward = group_response(lambda level: residual[level], inverse, vertical)
    message[0, 0:16, :] = upward
    message[0, 16:32, :] = downward
    coupling = group_rows(inverse, vertical)
    for row in range(3):
        message[0, 32 + row : 33 + row, :] = coupling[row]
    link = vertical[15:16, :]
    message[0, 35:36, :] = link * (link * inverse[1, 7, 7:8, :] - 1.0)
    message[0, 36:40, :] = jnp.zeros((4, LANES), F32)


def joined(first, last, *refs):
    refs = list(refs)
    flags, seg, got, inner = refs[:4]
    del refs[:4]
    if first:
        aux = refs.pop(0)
    else:
        terms = refs.pop(0)
    if last:
        own = refs.pop(0)
        if not first:
            ends = refs.pop(0)
        carried = refs.pop(0)
    else:
        seg_out, inner_out = refs.pop(0), refs.pop(0)
    if first:
        terms, aux_out = refs.pop(0), refs.pop(0)
        if last:
            ends = refs.pop(0)

    def row(ref, tile, index):
        return ref[tile, index : index + 1, :]

    def finish(tile, below, above_up, above_down):
        if last:
            leaving = row(ends, tile, 1) * below + own[tile, 0:16, :]
            carried[tile, 0:16, :] = below
            carried[tile, 16:32, :] = above_down + row(ends, tile, 0) * leaving
        else:
            inner_out[tile, 0:16, :] = below
            inner_out[tile, 16:32, :] = above_up
            inner_out[tile, 32:48, :] = above_down

    def prepare(tile, partner_below):
        for index in range(3):
            terms[tile, index : index + 1, :] = row(got, tile, 32 + index)
            terms[tile, 3 + index : 4 + index, :] = row(seg, tile, 32 + index)
        terms[tile, 6:7, :] = row(aux, tile, 0)
        terms[tile, 7:8, :] = row(aux, tile, 3)
        up_p, both_p, down_p, up, both, down = [row(terms, tile, index) for index in range(6)]
        below, above, through, back, flow = [row(aux, tile, index) for index in range(5)]
        if partner_below:
            bottom = jnp.broadcast_to(flags[1], flow.shape)
            flow = jnp.where(bottom == 1, row(got, tile, 35), flow)
            below = below * up_p
            joint = (up * up_p, both_p + down_p * both * up_p, down_p * down, row(seg, tile, 35))
        else:
            through = through + back * both_p * above
            above = up_p * above
            back = back * down_p
            joint = (up_p * up, both + down * both_p * up, down * down_p, row(got, tile, 35))
        for index, value in enumerate((below, above, through, back, flow)):
            aux_out[tile, index : index + 1, :] = value
        aux_out[tile, 5:8, :] = jnp.zeros((3, LANES), F32)
        if last:
            ends[tile, 0:1, :] = through
            ends[tile, 1:2, :] = row(own, tile, 32)
            ends[tile, 2:8, :] = jnp.zeros((6, LANES), F32)
        else:
            for index, value in enumerate(joint):
                seg_out[tile, 32 + index : 33 + index, :] = value
            seg_out[tile, 36:40, :] = jnp.zeros((4, LANES), F32)

    @pl.when(flags[0] == 1)
    def partner_below():
        for tile in range(GROUPS):
            if first:
                prepare(tile, True)
            came_up, came_down = got[tile, 0:16, :], got[tile, 16:32, :]
            if not last:
                upward, downward = seg[tile, 0:16, :], seg[tile, 16:32, :]
                seg_out[tile, 0:16, :] = row(terms, tile, 3) * came_up + upward
                seg_out[tile, 16:32, :] = came_down + row(terms, tile, 2) * (
                    downward + row(terms, tile, 4) * came_up
                )
            below = row(terms, tile, 6) * came_up + inner[tile, 0:16, :]
            finish(tile, below, inner[tile, 16:32, :], inner[tile, 32:48, :])

    @pl.when(flags[0] != 1)
    def partner_above():
        for tile in range(GROUPS):
            if first:
                prepare(tile, False)
            came_up, came_down = got[tile, 0:16, :], got[tile, 16:32, :]
            if not last:
                upward, downward = seg[tile, 0:16, :], seg[tile, 16:32, :]
                seg_out[tile, 0:16, :] = row(terms, tile, 0) * upward + came_up
                seg_out[tile, 16:32, :] = downward + row(terms, tile, 5) * (
                    came_down + row(terms, tile, 1) * upward
                )
            above_up, above_down = inner[tile, 16:32, :], inner[tile, 32:48, :]
            finish(
                tile,
                inner[tile, 0:16, :],
                row(terms, tile, 0) * above_up + came_up,
                above_down + row(terms, tile, 7) * (came_down + row(terms, tile, 1) * above_up),
            )


def solve_kernel(stage, last, *refs):
    refs = list(refs)

    def take(count):
        taken = refs[:count]
        del refs[:count]
        return taken

    count, inverse, vertical, residual_in, came = take(5)
    if stage:
        smoothed_in, applied, state_in = take(3)
        dot_parts = take(2)
    if stage == 2:
        solution_in, direction_in, image_in, flow_in, scalars_in = take(5)
    if stage:
        solution, residual, direction, scalars_out = take(4)
        if not last:
            image, flow, state = take(3)
    else:
        residual, state = residual_in, came
    smoothed, product = take(2)
    if not last:
        near, far, tables = take(3)
    (parts,) = take(1)
    tile = pl.program_id(0)
    rows, lanes = iotas()

    if stage:
        dots = dot_parts[0][...] + dot_parts[1][...]
        norm = jnp.sum(dots[0:1, :], axis=1, keepdims=True)
        curvature = jnp.sum(dots[1:2, :], axis=1, keepdims=True)
        if stage == 2:
            cross = jnp.sum(dots[2:3, :], axis=1, keepdims=True)
            ratio = norm / scalars_in[0:1, 0:1]
            curvature = curvature + ratio * cross + ratio * ratio * scalars_in[1:2, 0:1]
        step_size = norm / curvature
        scalars_out[0:1, :] = jnp.broadcast_to(norm, (1, LANES))
        scalars_out[1:2, :] = jnp.broadcast_to(curvature, (1, LANES))
        scalars_out[2:8, :] = jnp.zeros((6, LANES), F32)
        for level in range(LEVELS):
            value = smoothed_in[level]
            result = applied[level]
            if stage == 2:
                value = value + ratio * direction_in[level]
                result = result + ratio * image_in[level]
                solution[level] = solution_in[level] + step_size * value
            else:
                solution[level] = step_size * value
            direction[level] = value
            if not last:
                image[level] = result
            residual[level] = residual_in[level] - step_size * result
        change = came[0, 0:32, :]
        if stage == 2:
            change = change + ratio * flow_in[0]
        incoming = state_in[0, 0:32, :] - step_size * change
        if not last:
            flow[0] = change
            state[0] = incoming
    else:
        incoming = came[0, 0:32, :]
    link0, link1 = vertical[7:8, :], vertical[15:16, :]
    below = incoming[0:16]
    above = incoming[16:32]

    def block_product(block, lifted):
        solved = []
        for i in range(8):
            total = inverse[block, i, 0:1, :] * lifted[0]
            for j in range(1, 8):
                total = total + inverse[block, i, j : j + 1, :] * lifted[j]
            solved.append(total)
        return solved

    values = [residual[level] for level in range(8)]
    lower = block_product(0, [values[0] + below] + values[1:])
    values = [residual[8 + level] for level in range(8)]
    upper = block_product(1, [values[0] + link0 * lower[7]] + values[1:])
    lift = link1 * above
    upper = [upper[i] + lift * inverse[1, i, 7:8, :] for i in range(8)]
    lift = link0 * upper[0]
    lower = [lower[i] + lift * inverse[0, i, 7:8, :] for i in range(8)]
    total = None
    for level, value in enumerate(lower + upper):
        smoothed[level] = value
        term = value * residual[level]
        total = term if total is None else total + term

    @pl.when(tile == 0)
    def clear():
        parts[...] = jnp.zeros((16, LANES), F32)

    parts[...] += total

    @pl.when(tile == GROUPS - 1)
    def finish():
        product[...] = jnp.broadcast_to(jnp.sum(parts[...], axis=0, keepdims=True), product.shape)

    if last:
        return

    start = count[0] - LANES
    start_tile = lax.shift_right_logical(start, 7)
    offset = jnp.bitwise_and(start, LANES - 1)
    extra = start - 1
    extra_tile = lax.shift_right_logical(extra, 7)
    extra_lane = jnp.bitwise_and(extra, LANES - 1)
    in_tail = (tile == start_tile) | (tile == start_tile + 1)
    in_extra = tile == extra_tile

    def put(position, value):
        tables[position] = value

    @pl.when(in_tail | in_extra | (tile < 2))
    def build():
        store_tables(lambda level: smoothed[level], rows, put)

    def fill(tail, head):
        @pl.when(tile == 0)
        def clear_tail():
            tail[...] = jnp.zeros((25, 8, LANES), F32)
            head[...] = jnp.zeros((25, 8, LANES), F32)

        @pl.when(in_tail)
        def fill_tail():
            index = jnp.bitwise_and(lanes + offset, LANES - 1)
            before_wrap = (lanes < LANES - offset).astype(jnp.int32)
            wanted = before_wrap == (tile == start_tile).astype(jnp.int32)
            for position in range(24):
                tail[position] = jnp.where(
                    wanted, lane_take(tables[position], index), tail[position]
                )

        @pl.when(in_extra)
        def fill_extra():
            index = jnp.zeros_like(lanes) + extra_lane
            packed = jnp.zeros((8, LANES), F32)
            for position in range(24):
                packed = jnp.where(lanes == position, lane_take(tables[position], index), packed)
            tail[24] = packed

        @pl.when(tile == 0)
        def fill_head():
            for position in range(24):
                head[position] = tables[position]

        @pl.when(tile == 1)
        def fill_head_extra():
            packed = jnp.zeros((8, LANES), F32)
            for position in range(24):
                packed = jnp.where(
                    lanes == position, lane_take(tables[position], jnp.zeros_like(lanes)), packed
                )
            head[24] = packed

    odd = jnp.bitwise_and(count[1], 1)
    pl.when(odd == 0)(lambda: fill(near, far))
    pl.when(odd == 1)(lambda: fill(far, near))


def finish_kernel(norms, scalars_in, smoothed, direction_in, direction):
    ratio = total_of(norms[...]) / scalars_in[0:1, 0:1]
    for level in range(LEVELS):
        direction[level] = smoothed[level] + ratio * direction_in[level]


def split(values):
    high = values.astype(BF16)
    return high, (values - high.astype(F32)).astype(BF16)


def product3(tables, rows, columns, values):
    high, low = split(values)
    result = jnp.dot(tables[0, rows, columns], high, preferred_element_type=F32)
    result = result + jnp.dot(tables[0, rows, columns], low, preferred_element_type=F32)
    return result + jnp.dot(tables[1, rows, columns], high, preferred_element_type=F32)


def operate_kernel(
    helmholtz,
    plan,
    field,
    ints,
    copies,
    metric,
    mass,
    vertical,
    below_row,
    state,
    tables,
    applied,
    table,
    edges,
    corners,
    pick,
):
    tile = pl.program_id(0)
    rows, lanes = iotas()
    here = pl.ds(pl.multiple_of(tile * LANES, LANES), LANES)

    @pl.when(tile == 0)
    def build():
        def one(part, unused):
            there = pl.ds(pl.multiple_of(part * LANES, LANES), LANES)

            def put(position, value):
                table[position, :, there] = value

            store_tables(lambda level: field[level, :, there], rows, put)
            return unused

        lax.fori_loop(0, GROUPS, one, 0)

    gather_pick(table, 0, ints, plan, False, tile, edges, corners, pick)
    mixed, along_y, along_x = metric[1], metric[2], metric[0]
    for half in range(2):
        values = jnp.concatenate([field[8 * half + level, :, here] for level in range(8)], axis=0)
        gradients = product3(tables, slice(0, 256), slice(0, 128), values)
        flux_x = []
        flux_y = []
        for level in range(8):
            part_x = gradients[16 * level : 16 * level + 16]
            part_y = gradients[128 + 16 * level : 144 + 16 * level]
            flux_x.append(along_x * part_x + mixed * part_y)
            flux_y.append(mixed * part_x + along_y * part_y)
        stiff = product3(tables, slice(256, 384), slice(0, 256), jnp.concatenate(flux_x + flux_y, axis=0))
        for level in range(8):
            applied[8 * half + level] = stiff[16 * level : 16 * level + 16]
    twice = PENALTY * copies[...]
    flux = state[0, 0:16, :] + below_row[0, 4:5, :] * field[0, :, here]
    for level in range(LEVELS):
        value = field[level, :, here]
        higher = field[level + 1, :, here] if level < LEVELS - 1 else state[0, 16:32, :]
        next_flux = vertical[level : level + 1, :] * (value - higher)
        applied[level] = (
            applied[level]
            + (helmholtz[level] * mass[...] + twice) * value
            + (next_flux - flux)
            - PENALTY * pick[level]
        )
        flux = next_flux


def image_kernel(first, *refs):
    count, plan, applied, smoothed, ints, near, far, product, inverse, vertical = refs[:10]
    refs = refs[10:]
    if not first:
        direction, previous = refs[:2]
        refs = refs[2:]
    image, message, dots, table, edges, corners, pick, parts, crosses = refs
    tile = pl.program_id(0)
    rows, lanes = iotas()

    @pl.when(tile == 0)
    def build():
        parts[...] = jnp.zeros((16, LANES), F32)
        crosses[...] = jnp.zeros((16, LANES), F32)

        def fill(before, after):
            for position in range(24):
                index = jnp.full((8, LANES), position, jnp.int32)
                table[position, :, 0:LANES] = before[position]
                table[position, :, LANES : 2 * LANES] = after[position]
                table[position, :, 2 * LANES : 3 * LANES] = jnp.where(
                    lanes == 0, lane_take(before[24], index), lane_take(after[24], index)
                )

        odd = jnp.bitwise_and(count[1], 1)
        pl.when(odd == 0)(lambda: fill(far, near))
        pl.when(odd == 1)(lambda: fill(near, far))

    pick[...] = jnp.zeros((LEVELS, NODES, LANES), F32)

    @pl.when(plan[tile * PLAN + 1] > 0)
    def reach():
        gather_pick(table, 8, ints, plan, True, tile, edges, corners, pick)

    total = cross = None
    for level in range(LEVELS):
        value = smoothed[level]
        result = applied[level] - PENALTY * pick[level]
        image[level] = result
        term = value * result
        total = term if total is None else total + term
        if not first:
            term = value * previous[level] + direction[level] * result
            cross = term if cross is None else cross + term
    parts[...] += total
    if not first:
        crosses[...] += cross
    upward, downward = group_response(lambda level: image[level], inverse, vertical)
    message[0, 0:16, :] = upward
    message[0, 16:32, :] = downward

    @pl.when(tile == GROUPS - 1)
    def finish():
        dots[0:1, :] = product[0:1, :]
        dots[1:2, :] = jnp.sum(parts[...], axis=0, keepdims=True)
        dots[2:3, :] = jnp.sum(crosses[...], axis=0, keepdims=True)
        dots[3:8, :] = jnp.zeros((5, LANES), F32)


def field_spec():
    return pl.BlockSpec((LEVELS, NODES, LANES), lambda t: (0, 0, t))


def row_spec(rows):
    return pl.BlockSpec((rows, LANES), lambda t: (0, t))


def whole(*shape):
    return pl.BlockSpec(shape, lambda t: (0,) * len(shape))


def tile_spec(rows):
    return pl.BlockSpec((1, rows, LANES), lambda t: (t, 0, 0))


def inverse_spec():
    return pl.BlockSpec((2, 8, 8, LANES), lambda t: (0, 0, 0, t))


def scalars():
    return pl.BlockSpec(memory_space=pltpu.SMEM)


def struct(*shape):
    return jax.ShapeDtypeStruct(shape, F32)


def call(kernel, name, in_specs, out_specs, out_shape, scratch, cost, args):
    return pl.pallas_call(
        kernel,
        grid=(GROUPS,),
        in_specs=in_specs,
        out_specs=out_specs,
        out_shape=out_shape,
        scratch_shapes=scratch,
        name=name,
        compiler_params=pltpu.CompilerParams(
            dimension_semantics=("arbitrary",), vmem_limit_bytes=VMEM_BYTES
        ),
        cost_estimate=pl.CostEstimate(flops=cost, bytes_accessed=6 << 20, transcendentals=0),
    )(*args)


FIELD = (LEVELS, NODES, 1024)
PICK_SCRATCH = [
    ((4, LEVELS, 8, LANES), F32),
    ((4, 8, 8, LANES), F32),
    ((LEVELS, NODES, LANES), F32),
]


def vmem(shapes):
    return [pltpu.VMEM(shape, dtype) for shape, dtype in shapes]


def prepare_kernel(place, edge_rows, flip_rows, corner_rows, ints, copies):
    position, count_before = place[0], place[1]

    def source_of(entry):
        element = lax.shift_right_logical(entry, 2)
        holder = lax.shift_right_logical(element, 10)
        within = jnp.bitwise_and(element, 1023)
        earlier = within - (count_before - BORDER)
        earlier = jnp.where(earlier == 0, 10 * LANES, 8 * LANES + earlier - 1)
        later = jnp.where(within < LANES, 9 * LANES + within, 10 * LANES + 1)
        source = jnp.where(holder == position, within, jnp.where(holder < position, earlier, later))
        return jnp.where(entry >= 0, source, ABSENT)

    edges, corners = edge_rows[...], corner_rows[...]
    ints[0:4, :] = source_of(edges)
    ints[4:16, :] = source_of(corners)
    flipped = (flip_rows[...] == 1).astype(jnp.int32)
    straight = 2 * jnp.bitwise_and(edges, 3) + flipped
    swapped_row = 2 * jnp.bitwise_and(edges, 3) + 1 - flipped
    none = jnp.zeros((1, LANES), jnp.int32)

    def of(rows, side):
        return rows[side : side + 1, :]

    low = [none, of(straight, 0), of(swapped_row, 0), none, of(straight, 3), none, none, of(straight, 1)]
    high = [of(swapped_row, 3), none, none, of(swapped_row, 1), none, of(straight, 2),
            of(swapped_row, 2), none]
    for row, value in enumerate(low + high):
        ints[16 + row : 17 + row, :] = value
    ints[32:36, :] = jnp.zeros((4, LANES), jnp.int32)
    ints[36:48, :] = jnp.bitwise_and(corners, 3)
    on = (edges >= 0).astype(F32)
    there = (corners >= 0).astype(F32)
    shared = [
        of(there, 3 * corner) + of(there, 3 * corner + 1) + of(there, 3 * corner + 2)
        for corner in range(4)
    ]
    zero = jnp.zeros((1, LANES), F32)
    rows = [
        shared[0], of(on, 0), of(on, 0), shared[1], of(on, 3), zero, zero, of(on, 1),
        of(on, 3), zero, zero, of(on, 1), shared[3], of(on, 2), of(on, 2), shared[2],
    ]
    for row, value in enumerate(rows):
        copies[row : row + 1, :] = value


def gather_plan(ints):
    holder = (ints[:16] // LANES).reshape(16, 8, LANES)
    tiles = jnp.arange(11, dtype=jnp.int32)
    used = jnp.any(holder[:, :, None, :] == tiles[None, None, :, None], axis=(0, 3))
    far = tiles >= 8
    same = far[:, None] == far[None, :]
    earlier = used[:, None, :] & (same & (tiles[None, :] < tiles[:, None]))[None]
    place = jnp.sum(earlier.astype(jnp.int32), axis=2) + jnp.where(far, 10, 2)[None]
    columns = jnp.arange(PLAN, dtype=jnp.int32)
    listed = (place[:, :, None] == columns) * tiles[None, :, None]
    counted = columns[None, :] == jnp.where(far, 1, 0)[:, None]
    values = jnp.where(used[:, :, None], listed + counted[None].astype(jnp.int32), 0)
    return jnp.sum(values, axis=1).astype(jnp.int32).reshape(-1)


def parts_along(value, peers, inner):
    side = math.isqrt(peers)
    parts = []
    for shift in range(1, side):
        pairs = []
        for i in range(peers):
            outer, within = i // side, i % side
            if inner:
                pairs.append((i, outer * side + (within ^ shift)))
            else:
                pairs.append((i, (outer ^ shift) * side + within))
        parts.append(lax.ppermute(value, "elem", pairs))
    return parts


def swapped(value, distance):
    return lax.ppermute(value, "lev", [(i, i ^ distance) for i in range(GROUPS)])


def join(name, first, last, shapes, args):
    return pl.pallas_call(
        lambda *refs: joined(first, last, *refs),
        in_specs=[scalars()] + [pl.BlockSpec(memory_space=pltpu.VMEM)] * (len(args) - 1),
        out_shape=[struct(8, rows, LANES) for rows in shapes],
        name=name,
        cost_estimate=pl.CostEstimate(flops=1 << 16, bytes_accessed=1 << 18, transcendentals=0),
        compiler_params=pltpu.CompilerParams(vmem_limit_bytes=SMALL_VMEM_BYTES),
    )(*args)


def body(
    right_side,
    metric,
    mass_weight,
    helmholtz,
    vertical,
    block_inverse,
    edge_neighbour,
    edge_flip,
    corner_neighbour,
    element_count,
):
    peers = lax.axis_size("elem")
    position = lax.axis_index("elem")
    upward_elem = [(i, i + 1) for i in range(peers - 1)]
    near_pairs = [(i, i ^ 1) for i in range(peers)]
    far_pairs = [(i, i - 1 if i % 2 == 0 else i + 1) for i in range(1, peers - 1)]
    count = jnp.concatenate([element_count, position.astype(jnp.int32)[None]])

    residual, message = call(
        begin_kernel,
        "begin",
        [scalars(), field_spec(), inverse_spec(), row_spec(16)],
        [field_spec(), tile_spec(40)],
        [struct(*FIELD), struct(8, 40, LANES)],
        [],
        1 << 22,
        (element_count, right_side, block_inverse, vertical),
    )
    group = lax.axis_index("lev")
    flags = [
        jnp.stack([(group >> step) & 1, ((group & (2**step - 1)) == 0).astype(jnp.int32)])
        for step in range(3)
    ]
    ones = jnp.ones((8, 1, LANES), F32)
    nothing = jnp.zeros((8, 1, LANES), F32)
    aux = jnp.concatenate([ones, ones, nothing, ones] + [nothing] * 4, axis=1)
    empty = jnp.zeros((8, 48, LANES), F32)
    terms = [None] * 3
    seg, inner = message, empty
    for step in range(2):
        got = swapped(seg, 2**step)
        seg, inner, terms[step], aux = join(
            "join_first", True, False, [40, 48, 8, 8], (flags[step], seg, got, inner, aux)
        )
    got = swapped(seg, 4)
    came, terms[2], below_row, ends = join(
        "join_first_last", True, True, [32, 8, 8, 8], (flags[2], seg, got, inner, aux, message)
    )

    count_before = lax.ppermute(element_count, "elem", upward_elem)[0]
    ints, copies = call(
        prepare_kernel,
        "prepare",
        [scalars(), row_spec(4), row_spec(4), row_spec(12)],
        [row_spec(48), row_spec(16)],
        [jax.ShapeDtypeStruct((48, 1024), jnp.int32), struct(16, 1024)],
        [],
        1 << 18,
        (
            jnp.stack([position, count_before]).astype(jnp.int32),
            jnp.transpose(edge_neighbour),
            jnp.transpose(edge_flip),
            jnp.transpose(corner_neighbour, (1, 2, 0)).reshape(12, 1024),
        ),
    )
    plan = gather_plan(ints)
    tables = stacked_tables()

    shared_specs = [scalars(), inverse_spec(), row_spec(16), field_spec(), tile_spec(32)]
    halo = struct(25, 8, LANES)
    smoothed, product, near, far = call(
        lambda *refs: solve_kernel(0, False, *refs),
        "solve_first",
        shared_specs,
        [field_spec(), whole(8, LANES), whole(25, 8, LANES), whole(25, 8, LANES)],
        [struct(*FIELD), struct(8, LANES), halo, halo],
        vmem([((24, 8, LANES), F32), ((16, LANES), F32)]),
        1 << 22,
        (count, block_inverse, vertical, residual, came),
    )
    state = came
    solution = direction = image = flow = scalar_rows = None
    for iteration in range(ITERATIONS):
        first = iteration == 0
        last = iteration == ITERATIONS - 1
        near = lax.ppermute(near, "elem", near_pairs)
        far = lax.ppermute(far, "elem", far_pairs)
        applied = call(
            operate_kernel,
            "operate",
            [
                scalars(), scalars(), whole(*FIELD), row_spec(48), row_spec(16),
                pl.BlockSpec((3, NODES, LANES), lambda t: (0, 0, t)), row_spec(16), row_spec(16),
                tile_spec(8), tile_spec(32), whole(2, 384, 256),
            ],
            field_spec(),
            struct(*FIELD),
            vmem([((24, 8, 1024), F32)] + PICK_SCRATCH),
            1 << 30,
            (
                helmholtz, plan, smoothed, ints, copies, metric, mass_weight,
                vertical, below_row, state, tables,
            ),
        )
        args = [
            count, plan, applied, smoothed, ints, near, far, product, block_inverse,
            vertical,
        ]
        specs = [
            scalars(), scalars(), field_spec(), field_spec(), row_spec(48), whole(25, 8, LANES),
            whole(25, 8, LANES), whole(8, LANES), inverse_spec(), row_spec(16),
        ]
        if not first:
            args += [direction, image]
            specs += [field_spec(), field_spec()]
        applied, message, dots = call(
            lambda *refs, first=first: image_kernel(first, *refs),
            "image_first" if first else "image",
            specs,
            [field_spec(), tile_spec(32), whole(8, LANES)],
            [struct(*FIELD), struct(8, 32, LANES), struct(8, LANES)],
            vmem(
                [((24, 8, 3 * LANES), F32)] + PICK_SCRATCH + [((16, LANES), F32), ((16, LANES), F32)]
            ),
            1 << 22,
            args,
        )
        seg, inner = message, empty
        for step in range(2):
            got = swapped(seg, 2**step)
            others = parts_along(dots, peers, step == 0)
            got, *others = lax.optimization_barrier((got, *others))
            dots = (dots + others[0]) + (others[1] + others[2])
            seg, inner = join(
                "join", False, False, [32, 48], (flags[step], seg, got, inner, terms[step])
            )
        got = swapped(seg, 4)
        other = swapped(dots, 4)
        got, other = lax.optimization_barrier((got, other))
        dots = dots + other
        (came,) = join(
            "join_last", False, True, [32], (flags[2], seg, got, inner, terms[2], message, ends)
        )
        dots = dots + swapped(dots, 2)
        dots = [dots, swapped(dots, 1)]

        args = [count, block_inverse, vertical, residual, came, smoothed, applied, state] + dots
        specs = shared_specs + [field_spec(), field_spec(), tile_spec(32)] + [whole(8, LANES)] * 2
        if not first:
            args += [solution, direction, image, flow, scalar_rows]
            specs += [field_spec(), field_spec(), field_spec(), tile_spec(32), whole(8, LANES)]
        out_specs = [field_spec(), field_spec(), field_spec(), whole(8, LANES)]
        shapes = [struct(*FIELD), struct(*FIELD), struct(*FIELD), struct(8, LANES)]
        if last:
            out_specs += [field_spec(), whole(LANES, LANES)]
            shapes += [struct(*FIELD), struct(LANES, LANES)]
            scratch = vmem([((16, LANES), F32)])
        else:
            out_specs += [field_spec(), tile_spec(32), tile_spec(32), field_spec(), whole(8, LANES)]
            out_specs += [whole(25, 8, LANES), whole(25, 8, LANES)]
            shapes += [struct(*FIELD), struct(8, 32, LANES), struct(8, 32, LANES), struct(*FIELD)]
            shapes += [struct(8, LANES), halo, halo]
            scratch = vmem([((24, 8, LANES), F32), ((16, LANES), F32)])
        results = call(
            lambda *refs, first=first, last=last: solve_kernel(1 if first else 2, last, *refs),
            "solve_last" if last else "solve",
            specs,
            out_specs,
            shapes,
            scratch,
            1 << 22,
            args,
        )
        if last:
            solution, residual, direction, scalar_rows, smoothed, product = results
        else:
            solution, residual, direction, scalar_rows, image, flow, state = results[:7]
            smoothed, product, near, far = results[7:]
    norms = lax.all_to_all(product, ("elem", "lev"), split_axis=0, concat_axis=0, tiled=True)
    direction = call(
        finish_kernel,
        "finish",
        [whole(LANES, LANES), whole(8, LANES), field_spec(), field_spec()],
        field_spec(),
        struct(*FIELD),
        [],
        1 << 20,
        (norms, scalar_rows, smoothed, direction),
    )
    return (solution, residual, direction)


def solution(mesh):
    in_specs = (
        P("lev", None, "elem"),
        P(None, None, "elem"),
        P(None, "elem"),
        P("lev"),
        P("lev", "elem"),
        P("lev", None, None, "elem"),
        P("elem", None),
        P("elem", None),
        P("elem", None, None),
        P("elem"),
    )
    out_specs = (P("lev", None, "elem"), P("lev", None, "elem"), P("lev", None, "elem"))
    return jax.shard_map(body, mesh=mesh, in_specs=in_specs, out_specs=out_specs, check_vma=False)
```
